32 devices in a mesh: parts: 2 (over y), tensor: 16 (over z, x, core).
Axes of the slice: x: 2, y: 2, z: 4, core: 2. Of those that a mesh axis runs over, the one named last changes fastest.
Arguments:
- residual_input: bfloat16 [16, 8192], P('parts', 'tensor'), parts along dimension 0, may hold values from -42 to 42
- attention_norm_gain: bfloat16 [8192], P('tensor'), may hold values from 0.25 to 1.75
- wq: bfloat16 [8192, 8192], P('tensor'), may hold values from -0.0625 to 0.0625
- wk: bfloat16 [1024, 8192], P('tensor'), may hold values from -0.0625 to 0.0625
- wv: bfloat16 [1024, 8192], P('tensor'), may hold values from -0.0625 to 0.0625
- wo: bfloat16 [8192, 8192], P('tensor'), may hold values from -0.0625 to 0.0625
- query_down_factor: bfloat16 [32, 8192, 32], P(None, 'tensor'), may hold values from -0.0625 to 0.0625
- query_up_factor: bfloat16 [32, 32, 8192], P(None, None, 'tensor'), may hold values from -1 to 1
- value_down_factor: bfloat16 [32, 8192, 32], P(None, 'tensor'), may hold values from -0.0625 to 0.0625
- value_up_factor: bfloat16 [32, 32, 1024], P(None, None, 'tensor'), may hold values from -1 to 1
- request_adapter: int32 [16], P('parts'), parts along dimension 0, may hold values from 0 to 31
- cached_lengths: int32 [16], P('parts'), parts along dimension 0, may hold values from 2 to 512, as said below
- rotated_key_cache: bfloat16 [4096, 16, 128], P('tensor', 'parts'), parts along dimension 1, may hold values from -260 to 260
- cached_value_rows: bfloat16 [4096, 16, 128], P('tensor', 'parts'), parts along dimension 1, may hold values from -6 to 6
Outputs:
- states: bfloat16 [2, 16, 8192], P(None, 'parts', 'tensor'), parts along dimension 1
The draws below stay inside these ranges and needn't reach their ends.
There are 2 independent parts, one for each index of `parts`. The reference program is written for one: setup_inputs(seed, part) draws one part's arguments, and reference() takes and returns one part's arrays. A program takes and returns all parts, laid end to end along the dimension named above; an argument that names none is the same for every part. Nothing has to cross between parts.
Inputs may be any that keep to these rules, and one draw needn't show every extreme that they name: `cached_lengths`: at least one request has all 512 positions cached.
All inputs are finite; a program needn't handle non-finite values.
Results may differ from the reference program's by a relative error of at most 0.0062.
Values may be sent and summed in bfloat16 or wider, within the bound.
A program may use at most 128 MiB of HBM per device.

```python
import jax
import jax.numpy as jnp
from jax import lax

MODEL_WIDTH = 8192
QUERY_HEADS = 64
KEY_VALUE_HEADS = 8
HEAD_DIMENSION = 128
ADAPTER_RANK = 32
ADAPTERS_LOADED = 32
ROWS = 8
CTX_DEV = 256
STEPS = 2
SEQ_GROUPS = 2
CTX = 512


def draw_residual_input(key, part):
    key = jax.random.fold_in(key, 1)
    sample = jnp.clip(jax.random.normal(jax.random.fold_in(key, 1), (ROWS, MODEL_WIDTH), jnp.float32), -5.0, 5.0)
    col_scale = jnp.exp(jnp.log(3.0) * jnp.arange(MODEL_WIDTH, dtype=jnp.float32) / MODEL_WIDTH)
    sample = 0.7 * sample * col_scale[None, :]
    return sample.astype(jnp.bfloat16)


def draw_cached_lengths(key, part):
    key = jax.random.fold_in(key, 2)
    first_draw = jax.random.randint(jax.random.fold_in(key, 1), (ROWS,), 2, CTX + 1)
    second_draw = jax.random.randint(jax.random.fold_in(key, 2), (ROWS,), 2, CTX + 1)
    chosen_row = jax.random.randint(jax.random.fold_in(key, 3), (), 0, ROWS)
    lengths_drawn = jnp.minimum(first_draw, second_draw)
    return jnp.where(jnp.arange(ROWS) == chosen_row, CTX, lengths_drawn).astype(jnp.int32)


def draw_rotated_key_cache(key, part):
    key = jax.random.fold_in(key, 3)
    grid_shape = (KEY_VALUE_HEADS, CTX, ROWS, HEAD_DIMENSION)
    sample = jnp.clip(jax.random.normal(jax.random.fold_in(key, 1), grid_shape, jnp.float32), -6.0, 6.0)
    blocked = sample.reshape(KEY_VALUE_HEADS, SEQ_GROUPS, CTX_DEV, ROWS, HEAD_DIMENSION)
    blocked = jnp.transpose(blocked, (1, 0, 2, 3, 4))
    return blocked.reshape(KEY_VALUE_HEADS * CTX, ROWS, HEAD_DIMENSION).astype(jnp.bfloat16)


def with_ends(values, own_key, smallest, largest):
    index_at = [jax.random.randint(jax.random.fold_in(own_key, axis), (), 0, length) for axis, length in enumerate(values.shape)]
    longest = values.shape.index(max(values.shape))
    neighbour = index_at[:longest] + [(index_at[longest] + 1) % values.shape[longest]] + index_at[longest + 1:]
    return values.at[tuple(index_at)].set(smallest).at[tuple(neighbour)].set(largest)


def levels(stream_key, dims, split, smallest, largest):
    level, own = 1.0, jax.random.fold_in(stream_key, 6)
    for dim, blocks in split:
        steps = jnp.exp(jax.random.uniform(jax.random.fold_in(own, dim), (blocks,), jnp.float32, smallest / len(split), largest / len(split)))
        level = level * jnp.repeat(steps, dims[dim] // blocks).reshape([-1 if axis == dim else 1 for axis in range(len(dims))])
    return level


def centred(rng, dims, width, bound, shards=(), kind=jnp.bfloat16):
    values = jax.random.normal(rng, dims, jnp.float32) * width
    if len(shards) > 0:
        values = levels(rng, dims, shards, -0.22, 0.18) * values
    return jnp.clip(values, min=-bound, max=bound).astype(kind)


def setup_inputs(seed: int = 0, part: int = 0) -> dict:
    streams_of = jax.random.split(jax.random.key(seed), 15)
    part_splits = jax.random.split(jax.random.fold_in(streams_of[14], part), 15)
    return {
        "residual_input": draw_residual_input(jax.random.fold_in(jax.random.fold_in(streams_of[14], part), 71), part),
        "attention_norm_gain": jnp.clip(1.0 + 0.15 * jax.random.normal(streams_of[1], (MODEL_WIDTH,), jnp.float32), 0.25, 1.75).astype(jnp.bfloat16),
        "wq": centred(streams_of[2], (QUERY_HEADS * HEAD_DIMENSION, MODEL_WIDTH), MODEL_WIDTH ** -0.5, 0.0625, ((0, 16),)),
        "wk": centred(streams_of[3], (KEY_VALUE_HEADS * HEAD_DIMENSION, MODEL_WIDTH), MODEL_WIDTH ** -0.5, 0.0625, ((0, 16),)),
        "wv": centred(streams_of[4], (KEY_VALUE_HEADS * HEAD_DIMENSION, MODEL_WIDTH), MODEL_WIDTH ** -0.5, 0.0625, ((0, 16),)),
        "wo": centred(streams_of[5], (MODEL_WIDTH, QUERY_HEADS * HEAD_DIMENSION), (QUERY_HEADS * HEAD_DIMENSION) ** -0.5, 0.0625, ((0, 16),)),
        "query_down_factor": centred(streams_of[6], (ADAPTERS_LOADED, MODEL_WIDTH, ADAPTER_RANK), MODEL_WIDTH ** -0.5, 0.0625, ((1, 16),)),
        "query_up_factor": centred(streams_of[7], (ADAPTERS_LOADED, ADAPTER_RANK, QUERY_HEADS * HEAD_DIMENSION), ADAPTER_RANK ** -0.5, 1.0, ((2, 16),)),
        "value_down_factor": centred(streams_of[8], (ADAPTERS_LOADED, MODEL_WIDTH, ADAPTER_RANK), MODEL_WIDTH ** -0.5, 0.0625, ((1, 16),)),
        "value_up_factor": centred(streams_of[9], (ADAPTERS_LOADED, ADAPTER_RANK, KEY_VALUE_HEADS * HEAD_DIMENSION), ADAPTER_RANK ** -0.5, 1.0, ((2, 16),)),
        "request_adapter": with_ends(jax.random.randint(part_splits[10], (ROWS,), 0, ADAPTERS_LOADED), jax.random.fold_in(part_splits[10], 1), 0, ADAPTERS_LOADED - 1).astype(jnp.int32),
        "cached_lengths": draw_cached_lengths(jax.random.fold_in(jax.random.fold_in(streams_of[14], part), 71), part),
        "rotated_key_cache": draw_rotated_key_cache(jax.random.fold_in(jax.random.fold_in(streams_of[14], part), 71), part),
        "cached_value_rows": centred(part_splits[13], (KEY_VALUE_HEADS * CTX, ROWS, HEAD_DIMENSION), 1.0, 6.0, ((0, 16),)),
    }


theta_base = 500000.0
adapter_scale = 0.5
big_negative = -1e+30
eps_norm = 1e-05

def contract_final_axis(left, right):
    return lax.dot_general(left, right, (((1,), (1,)), ((), ())), preferred_element_type=jnp.float32)

def rotate_pairs(vectors, offset, positions):
    row_count, col_count = vectors.shape
    paired = vectors.reshape(row_count, col_count // 2, 2)
    pair_index = (offset // 2 + jnp.arange(col_count // 2, dtype=jnp.int32)) % (HEAD_DIMENSION // 2)
    frequency = jnp.power(jnp.float32(theta_base), -2.0 * pair_index.astype(jnp.float32) / HEAD_DIMENSION)
    angles = positions[:, None] * frequency[None, :]
    cosine = jnp.cos(angles)
    sine_part = jnp.sin(angles)
    even_part = paired[:, :, 0]
    odd_part = paired[:, :, 1]
    turned = jnp.stack([even_part * cosine - odd_part * sine_part, even_part * sine_part + odd_part * cosine], axis=2)
    return turned.reshape(row_count, col_count)

def adapter_down_project(normalized_input, adapter_indicator, factor):
    adapter_count, depth_rows, rank_size = factor.shape
    flat_table = jnp.transpose(factor, (1, 0, 2)).reshape(depth_rows, adapter_count * rank_size)
    spread = jnp.dot(normalized_input, flat_table, preferred_element_type=jnp.float32).reshape(-1, adapter_count, rank_size)
    return lax.optimization_barrier(jnp.sum(spread * adapter_indicator.astype(jnp.float32)[:, :, None], axis=1))

def adapter_row_select(shrink_low, adapter_indicator, factor):
    spread = (adapter_indicator[:, :, None] * shrink_low[:, None, :]).reshape(shrink_low.shape[0], -1)
    return jnp.dot(spread, factor.reshape(-1, factor.shape[2]), preferred_element_type=jnp.float32)

def head_major(cache_rows):
    blocked = cache_rows.reshape(SEQ_GROUPS, KEY_VALUE_HEADS, CTX_DEV, ROWS, HEAD_DIMENSION)
    return jnp.transpose(blocked, (1, 0, 2, 3, 4)).reshape(KEY_VALUE_HEADS, CTX, ROWS, HEAD_DIMENSION)

def reference(residual_input, attention_norm_gain, wq, wk, wv, wo, query_down_factor, query_up_factor, value_down_factor, value_up_factor, request_adapter, cached_lengths, rotated_key_cache, cached_value_rows):
    adapter_indicator = (request_adapter[:, None] == jnp.arange(ADAPTERS_LOADED, dtype=jnp.int32)[None, :]).astype(jnp.bfloat16)
    key_blocks = head_major(rotated_key_cache)
    value_blocks = head_major(cached_value_rows)
    cache_live = jnp.arange(CTX, dtype=jnp.int32)[None, :] < cached_lengths[:, None]
    per_group = QUERY_HEADS // KEY_VALUE_HEADS
    score_scale = HEAD_DIMENSION ** (-0.5)
    current = residual_input
    outputs = []
    fresh_keys = []
    fresh_values = []
    for step_index in range(STEPS):
        positions = (cached_lengths + step_index).astype(jnp.float32)
        widened = current.astype(jnp.float32)
        inv_rms = lax.rsqrt(lax.optimization_barrier(jnp.sum(widened * widened, axis=1)) / MODEL_WIDTH + eps_norm)
        normalized_input = (widened * inv_rms[:, None] * attention_norm_gain.astype(jnp.float32)[None, :]).astype(jnp.bfloat16)
        query_down_output = adapter_down_project(normalized_input, adapter_indicator, query_down_factor).astype(jnp.bfloat16)
        value_down_output = adapter_down_project(normalized_input, adapter_indicator, value_down_factor).astype(jnp.bfloat16)
        query_vector = contract_final_axis(normalized_input, wq) + adapter_scale * adapter_row_select(query_down_output, adapter_indicator, query_up_factor)
        query_vector = rotate_pairs(query_vector, 0, positions).astype(jnp.bfloat16)
        key_new = rotate_pairs(contract_final_axis(normalized_input, wk), 0, positions).astype(jnp.bfloat16)
        value_current = (contract_final_axis(normalized_input, wv) + adapter_scale * adapter_row_select(value_down_output, adapter_indicator, value_up_factor)).astype(jnp.bfloat16)
        fresh_keys.append(key_new.reshape(ROWS, KEY_VALUE_HEADS, HEAD_DIMENSION))
        fresh_values.append(value_current.reshape(ROWS, KEY_VALUE_HEADS, HEAD_DIMENSION))
        fresh_k = jnp.stack(fresh_keys, axis=2)
        fresh_v = jnp.stack(fresh_values, axis=2)
        grouped_q = query_vector.reshape(ROWS, KEY_VALUE_HEADS, per_group, HEAD_DIMENSION)

        def one_group(group_items):
            q_group, k_group, v_group, k_fresh, v_fresh = group_items
            q_wide = q_group.astype(jnp.float32)
            cached = jnp.einsum('bgd,pbd->bgp', q_wide, k_group.astype(jnp.float32)) * score_scale
            fresh_scores = jnp.einsum('bgd,bsd->bgs', q_wide, k_fresh.astype(jnp.float32)) * score_scale
            cached = jnp.where(cache_live[:, None, :], cached, big_negative)
            local_peak = jnp.maximum(lax.optimization_barrier(jnp.max(cached, axis=2)), lax.optimization_barrier(jnp.max(fresh_scores, axis=2)))
            cache_w = jnp.where(cache_live[:, None, :], jnp.exp(cached - local_peak[:, :, None]), 0.0)
            fresh_w = jnp.exp(fresh_scores - local_peak[:, :, None])
            local_total = lax.optimization_barrier(jnp.sum(cache_w, axis=2)) + lax.optimization_barrier(jnp.sum(fresh_w, axis=2))
            cache_low = cache_w.astype(jnp.bfloat16).astype(jnp.float32)
            fresh_low = fresh_w.astype(jnp.bfloat16).astype(jnp.float32)
            weighted = jnp.einsum('bgp,pbd->bgd', cache_low, v_group.astype(jnp.float32))
            weighted = weighted + jnp.einsum('bgs,bsd->bgd', fresh_low, v_fresh.astype(jnp.float32))
            return weighted / local_total[:, :, None]
        results = lax.map(one_group, (jnp.moveaxis(grouped_q, 1, 0), key_blocks, value_blocks, jnp.moveaxis(fresh_k, 1, 0), jnp.moveaxis(fresh_v, 1, 0)))
        attention = jnp.moveaxis(results, 0, 1).reshape(ROWS, QUERY_HEADS * HEAD_DIMENSION).astype(jnp.bfloat16)
        current = (widened + contract_final_axis(attention, wo)).astype(jnp.bfloat16)
        outputs.append(current)
    return jnp.stack(outputs, axis=0)
```

```python
import functools
import math

import jax
import jax.numpy as jnp
from jax import lax
from jax.experimental import pallas as pl
from jax.experimental.pallas import tpu as pltpu
from jax.sharding import PartitionSpec as P

MODEL_WIDTH = 8192
QUERY_HEADS = 64
KEY_VALUE_HEADS = 8
HEAD_DIMENSION = 128
STEPS = 2


theta_base = 500000.0
adapter_scale = 0.5
big_negative = -1e30
eps_norm = 1e-05


def merged(x, axis, combine):
    everything = jax.tree.map(
        lambda part, kind: lax.all_gather(part.astype(kind), axis),
        x,
        (jnp.bfloat16, jnp.bfloat16, jnp.bfloat16),
    )

    def take(k):
        return jax.tree.map(lambda part, own: part[k].astype(own.dtype), everything, x)

    return lax.fori_loop(
        1, lax.axis_size(axis), lambda k, so_far: combine(so_far, take(k)), take(0)
    )


def contract_final_axis(left, right):
    return lax.dot_general(
        left, right, (((1,), (1,)), ((), ())), preferred_element_type=jnp.float32
    )


def rotate_pairs(vectors, offset, positions):
    row_count, col_count = vectors.shape
    paired = vectors.reshape(row_count, col_count // 2, 2)
    pair_index = (offset // 2 + jnp.arange(col_count // 2, dtype=jnp.int32)) % (HEAD_DIMENSION // 2)
    frequency = jnp.power(
        jnp.float32(theta_base), -2.0 * pair_index.astype(jnp.float32) / HEAD_DIMENSION
    )
    angles = positions[:, None] * frequency[None, :]
    cosine = jnp.cos(angles)
    sine_part = jnp.sin(angles)
    even_part = paired[:, :, 0]
    odd_part = paired[:, :, 1]
    turned = jnp.stack(
        [even_part * cosine - odd_part * sine_part, even_part * sine_part + odd_part * cosine],
        axis=2,
    )
    return turned.reshape(row_count, col_count)


def adapter_down_project(normalized_input, adapter_indicator, factor):
    adapter_count, depth_rows, rank_size = factor.shape
    flat_table = jnp.transpose(factor, (1, 0, 2)).reshape(depth_rows, adapter_count * rank_size)
    spread = jnp.dot(normalized_input, flat_table, preferred_element_type=jnp.float32).reshape(
        -1, adapter_count, rank_size
    )
    return jnp.sum(spread * adapter_indicator.astype(jnp.float32)[:, :, None], axis=1)


def adapter_row_select(shrink_low, adapter_indicator, factor):
    spread = (adapter_indicator[:, :, None] * shrink_low[:, None, :]).reshape(
        shrink_low.shape[0], -1
    )
    return jnp.dot(spread, factor.reshape(-1, factor.shape[2]), preferred_element_type=jnp.float32)


def combine_parts(earlier, later):
    peak_one, total_one, summed_one = earlier
    peak_two, total_two, summed_two = later
    peak_both = jnp.maximum(peak_one, peak_two)
    scale_one = jnp.exp(peak_one - peak_both)
    scale_two = jnp.exp(peak_two - peak_both)
    row_count, head_count = peak_one.shape
    head_size = summed_one.shape[1] // head_count
    summed_both = summed_one.reshape(row_count, head_count, head_size) * scale_one[:, :, None]
    summed_both = (
        summed_both + summed_two.reshape(row_count, head_count, head_size) * scale_two[:, :, None]
    )
    return (
        peak_both,
        total_one * scale_one + total_two * scale_two,
        summed_both.reshape(row_count, head_count * head_size),
    )


def local(
    residual_input,
    attention_norm_gain,
    wq,
    wk,
    wv,
    wo,
    query_down_factor,
    query_up_factor,
    value_down_factor,
    value_up_factor,
    request_adapter,
    cached_lengths,
    rotated_key_cache,
    cached_value_rows,
):
    my_index = lax.axis_index("tensor")
    kv_group = my_index % KEY_VALUE_HEADS
    seq_block = my_index // KEY_VALUE_HEADS
    row_count, local_width = residual_input.shape
    ctx_dev = rotated_key_cache.shape[0]
    q_cols = wq.shape[0]
    kv_cols = wk.shape[0]
    per_group = QUERY_HEADS // KEY_VALUE_HEADS
    score_scale = HEAD_DIMENSION ** (-0.5)
    adapter_indicator = (
        request_adapter[:, None] == jnp.arange(query_down_factor.shape[0], dtype=jnp.int32)[None, :]
    ).astype(jnp.bfloat16)
    cache_pos = seq_block * ctx_dev + jnp.arange(ctx_dev, dtype=jnp.int32)
    cache_live = cache_pos[None, :] < cached_lengths[:, None]
    first_block = seq_block == 0
    group_mask = jnp.arange(KEY_VALUE_HEADS, dtype=jnp.int32) == kv_group
    group_float = group_mask.astype(jnp.float32)
    current = residual_input
    outputs = []
    fresh_keys = []
    fresh_values = []
    for step_index in range(STEPS):
        positions = (cached_lengths + step_index).astype(jnp.float32)
        widened = current.astype(jnp.float32)
        squares = lax.psum(jnp.sum(widened * widened, axis=1), "tensor")
        inv_rms = lax.rsqrt(squares / MODEL_WIDTH + eps_norm)
        local_normalized = (
            widened * inv_rms[:, None] * attention_norm_gain.astype(jnp.float32)[None, :]
        ).astype(jnp.bfloat16)
        part_rows = lax.all_gather(local_normalized, "tensor", axis=1, tiled=True)
        query_sum = contract_final_axis(part_rows, wq)
        k_sum = contract_final_axis(part_rows, wk)
        value_sum = contract_final_axis(part_rows, wv)
        query_down_output, value_down_output = lax.psum(
            (
                adapter_down_project(local_normalized, adapter_indicator, query_down_factor),
                adapter_down_project(local_normalized, adapter_indicator, value_down_factor),
            ),
            "tensor",
        )
        query_vector = query_sum + adapter_scale * adapter_row_select(
            query_down_output.astype(jnp.bfloat16), adapter_indicator, query_up_factor
        )
        query_vector = rotate_pairs(query_vector, my_index * q_cols, positions).astype(jnp.bfloat16)
        key_new = rotate_pairs(k_sum, my_index * kv_cols, positions).astype(jnp.bfloat16)
        value_current = (
            value_sum
            + adapter_scale
            * adapter_row_select(
                value_down_output.astype(jnp.bfloat16), adapter_indicator, value_up_factor
            )
        ).astype(jnp.bfloat16)
        full_q, full_k, full_v = (
            lax.all_gather(query_vector, "tensor", axis=1, tiled=True),
            lax.all_gather(key_new, "tensor", axis=1, tiled=True),
            lax.all_gather(value_current, "tensor", axis=1, tiled=True),
        )
        group_q = lax.dynamic_slice_in_dim(
            full_q, kv_group * per_group * HEAD_DIMENSION, per_group * HEAD_DIMENSION, 1
        ).reshape(row_count, per_group, HEAD_DIMENSION)
        fresh_keys.append(
            lax.dynamic_slice_in_dim(full_k, kv_group * HEAD_DIMENSION, HEAD_DIMENSION, 1)
        )
        fresh_values.append(
            lax.dynamic_slice_in_dim(full_v, kv_group * HEAD_DIMENSION, HEAD_DIMENSION, 1)
        )
        fresh_k = jnp.stack(fresh_keys, axis=1)
        fresh_v = jnp.stack(fresh_values, axis=1)
        cached = (
            jnp.einsum(
                "bgd,pbd->bgp", group_q, rotated_key_cache, preferred_element_type=jnp.float32
            )
            * score_scale
        )
        fresh_scores = (
            jnp.einsum("bgd,bsd->bgs", group_q, fresh_k, preferred_element_type=jnp.float32)
            * score_scale
        )
        cached = jnp.where(cache_live[:, None, :], cached, big_negative)
        fresh_scores = jnp.where(first_block, fresh_scores, big_negative)
        local_peak = jnp.maximum(jnp.max(cached, axis=2), jnp.max(fresh_scores, axis=2))
        cache_w = jnp.where(cache_live[:, None, :], jnp.exp(cached - local_peak[:, :, None]), 0.0)
        fresh_w = jnp.where(first_block, jnp.exp(fresh_scores - local_peak[:, :, None]), 0.0)
        local_total = jnp.sum(cache_w, axis=2) + jnp.sum(fresh_w, axis=2)
        weighted = jnp.einsum(
            "bgp,pbd->bgd",
            cache_w.astype(jnp.bfloat16),
            cached_value_rows,
            preferred_element_type=jnp.float32,
        )
        weighted = weighted + jnp.einsum(
            "bgs,bsd->bgd",
            fresh_w.astype(jnp.bfloat16),
            fresh_v,
            preferred_element_type=jnp.float32,
        )
        maxima = jnp.where(group_mask[None, :, None], local_peak[:, None, :], big_negative).reshape(
            row_count, QUERY_HEADS
        )
        totals = (group_float[None, :, None] * local_total[:, None, :]).reshape(
            row_count, QUERY_HEADS
        )
        values_all = (group_float[None, :, None, None] * weighted[:, None, :, :]).reshape(
            row_count, QUERY_HEADS * HEAD_DIMENSION
        )
        peak_all, denominator, summed = merged(
            (maxima, totals, values_all), "tensor", combine_parts
        )
        attention = (
            (summed.reshape(row_count, QUERY_HEADS, HEAD_DIMENSION) / denominator[:, :, None])
            .reshape(row_count, QUERY_HEADS * HEAD_DIMENSION)
            .astype(jnp.bfloat16)
        )
        projected = contract_final_axis(attention, wo)
        current = (widened + projected).astype(jnp.bfloat16)
        outputs.append(current)
    return jnp.stack(outputs, axis=0)


def fused_kernel(
    n,
    ctx_dev,
    current_ref,
    gain_ref,
    adapter_ref,
    length_ref,
    wq_hbm,
    wk_hbm,
    wv_hbm,
    wo_hbm,
    qd_hbm,
    qu_hbm,
    vd_hbm,
    vu_hbm,
    kc_hbm,
    vc_hbm,
    out_ref,
    w_s,
    wo_s,
    qd_s,
    vd_s,
    qu_s,
    vu_s,
    k_s,
    v_s,
    dq_s,
    dv_s,
    uq_s,
    uv_s,
    xg,
    sg,
    qg,
    og,
    xsend,
    ssend,
    qsend,
    osend,
    norm_s,
    attn_s,
    gain_s,
    load_sem,
    x_send_sem,
    x_recv_sem,
    s_send_sem,
    s_recv_sem,
    q_send_sem,
    q_recv_sem,
    o_send_sem,
    o_recv_sem,
):
    f32, bf16 = jnp.float32, jnp.bfloat16
    hd, groups = HEAD_DIMENSION, KEY_VALUE_HEADS
    rows, width = current_ref.shape
    q_cols, kv_cols = wq_hbm.shape[0], wk_hbm.shape[0]
    chunks = width // hd
    heads_here = q_cols // hd
    per_group = QUERY_HEADS // groups
    blocks = n // groups
    cached_rows = ctx_dev * rows
    rank = qd_hbm.shape[1]
    me = lax.axis_index("tensor")

    loads = []

    def load(src, dst):
        copy = pltpu.make_async_copy(src, dst, load_sem.at[len(loads)])
        copy.start()
        loads.append(copy)
        return copy

    small = [
        load(qd_hbm, qd_s),
        load(vd_hbm, vd_s),
    ]
    pieces = 4
    step_cols = MODEL_WIDTH // pieces
    weights = []
    for piece in range(pieces):
        cols = pl.ds(piece * step_cols, step_cols)
        weights.append(
            [
                load(wq_hbm.at[:, cols], w_s.at[pl.ds(0, q_cols), cols]),
                load(wk_hbm.at[:, cols], w_s.at[pl.ds(q_cols, kv_cols), cols]),
                load(wv_hbm.at[:, cols], w_s.at[pl.ds(q_cols + kv_cols, kv_cols), cols]),
            ]
        )
    ups = [load(qu_hbm, qu_s), load(vu_hbm, vu_s)]
    caches = [
        load(kc_hbm, k_s.at[pl.ds(0, cached_rows)]),
        load(vc_hbm, v_s.at[pl.ds(0, cached_rows)]),
    ]
    out_weights = []
    for piece in range(pieces):
        cols = pl.ds(piece * step_cols, step_cols)
        out_weights.append(load(wo_hbm.at[:, cols], wo_s.at[:, cols]))

    barrier = pltpu.get_barrier_semaphore()

    def greet(k, carry):
        pl.semaphore_signal(
            barrier,
            inc=1,
            device_id={"tensor": lax.rem(me + k, n)},
            device_id_type=pl.DeviceIdType.MESH,
        )
        return carry

    lax.fori_loop(1, n, greet, 0)

    def remote(src, dst, send_sem, recv_sem, target):
        return pltpu.make_async_remote_copy(
            src_ref=src,
            dst_ref=dst,
            send_sem=send_sem,
            recv_sem=recv_sem,
            device_id={"tensor": target},
            device_id_type=pl.DeviceIdType.MESH,
        )

    def for_others(body):
        def step(k, carry):
            body(lax.rem(me + k, n))
            return carry

        lax.fori_loop(1, n, step, 0)

    def x_copy(t, slot, target):
        size = xsend.shape[1] if t == 0 else chunks * rows
        return remote(
            xsend.at[t, pl.ds(0, size)],
            xg.at[t, slot, pl.ds(0, size)],
            x_send_sem.at[t, target],
            x_recv_sem.at[t, slot],
            target,
        )

    def s_copy(t, slot, target):
        return remote(
            ssend.at[t], sg.at[t, slot], s_send_sem.at[t, target], s_recv_sem.at[t, slot], target
        )

    def o_copy(t, slot, target):
        return remote(
            osend.at[t], og.at[t, slot], o_send_sem.at[t, target], o_recv_sem.at[t, slot], target
        )

    def q_copy(t, slot, block, target):
        return remote(
            qsend.at[t], qg.at[t, slot], q_send_sem.at[t, block], q_recv_sem.at[t, slot], target
        )

    lane = lax.broadcasted_iota(jnp.int32, (rows, hd), 1)
    row = lax.broadcasted_iota(jnp.int32, (rows, hd), 0)
    gains = gain_ref[...]
    row16 = lax.broadcasted_iota(jnp.int32, (16, hd), 0)

    def split_chunks(x):
        return [x[:, c * hd : (c + 1) * hd] for c in range(x.shape[1] // hd)]

    current = current_ref[...].astype(f32)
    gain16 = jnp.zeros((16, hd), f32)
    for c, piece in enumerate(split_chunks(gains)):
        gain16 = jnp.where(row16 == c, piece[0:1, :], gain16)

    def send_state(t):
        parts = split_chunks(current) + ([gain16] if t == 0 else [])
        message = jnp.concatenate(parts, axis=0).astype(bf16)
        xsend[t, pl.ds(0, message.shape[0])] = message
        xg[t, me, pl.ds(0, message.shape[0])] = message
        if t == 0:
            pl.semaphore_wait(barrier, n - 1)
        for_others(lambda target: x_copy(t, me, target).start())

    send_state(0)

    lengths = jnp.zeros((rows, hd), jnp.int32)
    for r in range(rows):
        lengths = jnp.where(row == r, length_ref[r], lengths)
    lane_even = lax.rem(lane, 2) == 0

    def angle_tables(pair, positions):
        frequency = jnp.exp(pair.astype(f32) * jnp.float32(-2.0 * math.log(theta_base) / hd))
        angles = positions * frequency
        sine = jnp.sin(angles)
        return jnp.cos(angles), jnp.where(lane_even, -sine, sine)

    fresh_pair = lax.rem(me, 2) * (kv_cols // 2) + lax.rem(lane, kv_cols) // 2
    is_key = lane < kv_cols
    tables = []
    for t in range(STEPS):
        positions = (lengths + t).astype(f32)
        q_cos, q_sin = angle_tables(lane // 2, positions)
        k_cos, k_sin = angle_tables(fresh_pair, positions)
        tables.append(
            (q_cos, q_sin, jnp.where(is_key, k_cos, 1.0), jnp.where(is_key, k_sin, 0.0))
        )

    def rotate(x, cosine, sine):
        swapped = jnp.where(lane_even, pltpu.roll(x, hd - 1, 1), pltpu.roll(x, 1, 1))
        return x * cosine + swapped * sine

    extra = k_s.shape[0] - cached_rows
    k_s[pl.ds(cached_rows, extra)] = jnp.zeros((extra, hd), bf16)
    v_s[pl.ds(cached_rows, extra)] = jnp.zeros((extra, hd), bf16)

    column = lax.broadcasted_iota(jnp.int32, (rows, cached_rows + extra), 1)
    wide_row = lax.broadcasted_iota(jnp.int32, (rows, cached_rows + extra), 0)
    seq_block = me // groups
    wide_length = jnp.zeros((rows, cached_rows + extra), jnp.int32)
    for r in range(rows):
        wide_length = jnp.where(wide_row == r, length_ref[r], wide_length)
    own_cached = (
        (column < cached_rows)
        & (lax.rem(column, rows) == wide_row)
        & (seq_block * ctx_dev + column // rows < wide_length)
    )
    fresh_column = column - cached_rows
    fresh_row = (fresh_column >= 0) & (lax.rem(column, 16) == wide_row) & (seq_block == 0)

    for copy in small:
        copy.wait()
    for r in range(rows):
        adapter = adapter_ref[r]
        dq_s[pl.ds(r * rank, rank)] = qd_s[adapter]
        dv_s[pl.ds(r * rank, rank)] = vd_s[adapter]

    spread_column = lax.broadcasted_iota(jnp.int32, (rows, rows * rank), 1)
    spread_row = lax.broadcasted_iota(jnp.int32, (rows, rows * rank), 0)
    own_block = spread_column // rank == spread_row
    even_block = lax.rem(lane // rank, 2) == 0

    def contract(left, right):
        return lax.dot_general(
            left, right, (((1,), (1,)), ((), ())), preferred_element_type=f32
        )

    def fold(x):
        x = jnp.where(own_block, x, 0.0)
        parts = split_chunks(x)
        total = parts[0]
        for part in parts[1:]:
            total = total + part
        shift = hd // 2
        while shift >= rank:
            total = total + pltpu.roll(total, shift, 1)
            shift //= 2
        return total

    def send_shrink(t):
        scaled = (current * gains).astype(bf16)
        both = jnp.where(
            even_block, fold(contract(scaled, dq_s[...])), fold(contract(scaled, dv_s[...]))
        )
        ssend[t] = both
        sg[t, me] = both
        for_others(lambda target: s_copy(t, me, target).start())

    send_shrink(0)

    for t in range(STEPS):
        for_others(lambda source: x_copy(t, source, source).wait_recv())
        squares = jnp.zeros((rows, hd), f32)
        for d in range(n):
            block = xg[t, d, pl.ds(0, chunks * rows)].astype(f32)
            for c in range(chunks):
                part = block[c * rows : (c + 1) * rows]
                squares = squares + part * part
            if t == 0:
                gain_block = xg[0, d, pl.ds(chunks * rows, 16)].astype(f32)
                gain_s[pl.ds(d * chunks, chunks)] = gain_block[0:chunks]
        total = jnp.sum(squares, axis=1, keepdims=True)
        inv_rms = lax.rsqrt(total / MODEL_WIDTH + eps_norm)
        for d in range(n):
            block = xg[t, d, pl.ds(0, chunks * rows)].astype(f32)
            for c in range(chunks):
                at = d * chunks + c
                part = block[c * rows : (c + 1) * rows]
                normed = part * inv_rms * gain_s[pl.ds(at, 1)]
                norm_s[:, pl.ds(at * hd, hd)] = normed.astype(bf16)
        products = jnp.zeros((rows, q_cols + 2 * kv_cols), f32)
        for piece in range(pieces):
            cols = pl.ds(piece * step_cols, step_cols)
            if t == 0:
                for copy in weights[piece]:
                    copy.wait()
            products = products + contract(norm_s[:, cols], w_s[:, cols])
        if t == 0:
            for copy in ups:
                copy.wait()
            for r in range(rows):
                adapter = adapter_ref[r]
                uq_s[pl.ds(r * rank, rank)] = qu_s[adapter]
                uv_s[pl.ds(r * rank, rank)] = vu_s[adapter]
        for_others(lambda source: s_copy(t, source, source).wait_recv())
        shrink = sg[t, 0]
        for d in range(1, n):
            shrink = shrink + sg[t, d]
        shrink = shrink * inv_rms
        turned = pltpu.roll(shrink, rank, 1)

        def spread(x):
            x = jnp.concatenate([x] * (rows * rank // hd), axis=1)
            return jnp.where(own_block, x, 0.0).astype(bf16)

        q_low = spread(jnp.where(even_block, shrink, turned))
        v_low = spread(jnp.where(even_block, turned, shrink))
        q_up = jnp.dot(q_low, uq_s[...], preferred_element_type=f32)
        v_up = jnp.dot(v_low, uv_s[...], preferred_element_type=f32)
        query = products[:, :q_cols] + adapter_scale * q_up
        fresh = products[:, q_cols:] + adapter_scale * jnp.concatenate(
            [jnp.zeros((rows, kv_cols), f32), v_up], axis=1
        )
        q_cos, q_sin, k_cos, k_sin = tables[t]
        parts = [rotate(part, q_cos, q_sin) for part in split_chunks(query)]
        parts.append(rotate(fresh, k_cos, k_sin))
        parts.append(jnp.zeros((rows, hd), f32))
        message = jnp.concatenate(parts, axis=0).astype(bf16)
        qsend[t] = message
        side = lax.rem(me, 2)
        for block in range(blocks):
            target = me // 2 + block * groups

            @pl.when(target == me)
            def _():
                qg[t, side] = message

            @pl.when(target != me)
            def _():
                q_copy(t, side, block, target).start()

        if t == 0:
            for copy in caches:
                copy.wait()
        for half in range(2):
            source = 2 * lax.rem(me, groups) + half

            @pl.when(source != me)
            def _():
                q_copy(t, half, 0, source).wait_recv()

        first = qg[t, 0].astype(f32)
        second = qg[t, 1].astype(f32)
        q_rows = heads_here * rows
        queries = jnp.concatenate([first[:q_rows], second[:q_rows]], axis=0).astype(bf16)
        first_kv = first[q_rows : q_rows + rows]
        second_kv = second[q_rows : q_rows + rows]
        key_new = jnp.where(is_key, first_kv, pltpu.roll(second_kv, kv_cols, 1))
        value_new = jnp.where(is_key, pltpu.roll(first_kv, kv_cols, 1), second_kv)
        blank = jnp.zeros((16 - rows, hd), f32)
        k_s[pl.ds(cached_rows + 16 * t, 16)] = jnp.concatenate([key_new, blank], 0).astype(bf16)
        v_s[pl.ds(cached_rows + 16 * t, 16)] = jnp.concatenate([value_new, blank], 0).astype(bf16)
        scores = contract(queries, k_s[...]) * (HEAD_DIMENSION ** (-0.5))
        scores = scores.reshape(per_group, rows, cached_rows + extra)
        live = (own_cached | (fresh_row & (fresh_column < 16 * (t + 1))))[None]
        scores = jnp.where(live, scores, big_negative)
        peak = jnp.max(scores, axis=2, keepdims=True)
        weight = jnp.where(live, jnp.exp(scores - peak), 0.0)
        mass = jnp.sum(weight, axis=2, keepdims=True)
        weight = weight.reshape(per_group * rows, cached_rows + extra).astype(bf16)
        summed = jnp.dot(weight, v_s[...], preferred_element_type=f32)
        summed = summed.reshape(per_group, rows, hd)
        some = mass > 0.0
        safe = jnp.where(some, mass, 1.0)
        partial = summed / safe
        level = jnp.where(some, peak + jnp.log(safe), big_negative)
        levels = jnp.zeros((rows, hd), f32)
        for h in range(per_group):
            levels = jnp.where(lane == h, level[h], levels)
        high = levels.astype(bf16).astype(f32)
        middle = (levels - high).astype(bf16).astype(f32)
        low = levels - high - middle
        packed = high + pltpu.roll(middle, per_group, 1) + pltpu.roll(low, 2 * per_group, 1)
        message = jnp.concatenate(
            [partial.reshape(per_group * rows, hd), packed, jnp.zeros((16 - rows, hd), f32)], axis=0
        ).astype(bf16)
        osend[t] = message
        og[t, me] = message
        for_others(lambda target: o_copy(t, me, target).start())
        for_others(lambda source: o_copy(t, source, source).wait_recv())
        for g in range(groups):
            found = []
            for b in range(blocks):
                entry = og[t, b * groups + g].astype(f32)
                packed = entry[per_group * rows : per_group * rows + rows]
                level = (
                    packed
                    + pltpu.roll(packed, hd - per_group, 1)
                    + pltpu.roll(packed, hd - 2 * per_group, 1)
                )
                found.append((level, entry))
            top = found[0][0]
            for level, _ in found[1:]:
                top = jnp.maximum(top, level)
            shares = [jnp.exp(level - top) for level, _ in found]
            whole = shares[0]
            for share in shares[1:]:
                whole = whole + share
            for h in range(per_group):
                value = jnp.zeros((rows, hd), f32)
                for share, (_, entry) in zip(shares, found):
                    part = (share / whole)[:, h : h + 1]
                    value = value + part * entry[h * rows : (h + 1) * rows]
                attn_s[:, pl.ds((g * per_group + h) * hd, hd)] = value.astype(bf16)
        projected = jnp.zeros((rows, width), f32)
        for piece in range(pieces):
            cols = pl.ds(piece * step_cols, step_cols)
            if t == 0:
                out_weights[piece].wait()
            projected = projected + contract(attn_s[:, cols], wo_s[:, cols])
        rounded = (current + projected).astype(bf16)
        out_ref[t] = rounded
        current = rounded.astype(f32)
        if t + 1 < STEPS:
            send_state(t + 1)
            send_shrink(t + 1)

    for t in range(STEPS):
        for_others(lambda target: x_copy(t, me, target).wait_send())
        for_others(lambda target: s_copy(t, me, target).wait_send())
        for_others(lambda target: o_copy(t, me, target).wait_send())
        for block in range(blocks):
            target = me // 2 + block * groups

            @pl.when(target != me)
            def _():
                q_copy(t, 0, block, target).wait_send()


def fused(
    n,
    residual_input,
    attention_norm_gain,
    wq,
    wk,
    wv,
    wo,
    query_down_factor,
    query_up_factor,
    value_down_factor,
    value_up_factor,
    request_adapter,
    cached_lengths,
    rotated_key_cache,
    cached_value_rows,
):
    rows, width = residual_input.shape
    ctx_dev = rotated_key_cache.shape[0]
    q_cols, kv_cols = wq.shape[0], wk.shape[0]
    adapters, _, rank = query_down_factor.shape
    hd = HEAD_DIMENSION
    chunks = width // hd
    per_group = QUERY_HEADS // KEY_VALUE_HEADS
    blocks = n // KEY_VALUE_HEADS
    kv_rows = ctx_dev * rows + 128
    x_rows = chunks * rows + 16
    q_rows = (q_cols // hd + 2) * rows
    o_rows = per_group * rows + 16
    bf16, f32 = jnp.bfloat16, jnp.float32
    dma = pltpu.SemaphoreType.DMA
    any_spec = pl.BlockSpec(memory_space=pl.ANY)
    vmem = pl.BlockSpec(memory_space=pltpu.VMEM)
    smem = pl.BlockSpec(memory_space=pltpu.SMEM)
    return pl.pallas_call(
        functools.partial(fused_kernel, n, ctx_dev),
        out_shape=jax.ShapeDtypeStruct((STEPS, rows, width), bf16),
        in_specs=[vmem, vmem, smem, smem] + [any_spec] * 10,
        out_specs=vmem,
        scratch_shapes=[
            pltpu.VMEM((q_cols + 2 * kv_cols, MODEL_WIDTH), bf16),
            pltpu.VMEM((width, MODEL_WIDTH), bf16),
            pltpu.VMEM((adapters, rank, width), bf16),
            pltpu.VMEM((adapters, rank, width), bf16),
            pltpu.VMEM((adapters, rank, q_cols), bf16),
            pltpu.VMEM((adapters, rank, kv_cols), bf16),
            pltpu.VMEM((kv_rows, hd), bf16),
            pltpu.VMEM((kv_rows, hd), bf16),
            pltpu.VMEM((rows * rank, width), bf16),
            pltpu.VMEM((rows * rank, width), bf16),
            pltpu.VMEM((rows * rank, q_cols), bf16),
            pltpu.VMEM((rows * rank, kv_cols), bf16),
            pltpu.VMEM((STEPS, n, x_rows, hd), bf16),
            pltpu.VMEM((STEPS, n, rows, hd), f32),
            pltpu.VMEM((STEPS, 2, q_rows, hd), bf16),
            pltpu.VMEM((STEPS, n, o_rows, hd), bf16),
            pltpu.VMEM((STEPS, x_rows, hd), bf16),
            pltpu.VMEM((STEPS, rows, hd), f32),
            pltpu.VMEM((STEPS, q_rows, hd), bf16),
            pltpu.VMEM((STEPS, o_rows, hd), bf16),
            pltpu.VMEM((rows, MODEL_WIDTH), bf16),
            pltpu.VMEM((rows, QUERY_HEADS * hd), bf16),
            pltpu.VMEM((MODEL_WIDTH // hd, hd), f32),
            dma((24,)),
            dma((STEPS, n)),
            dma((STEPS, n)),
            dma((STEPS, n)),
            dma((STEPS, n)),
            dma((STEPS, blocks)),
            dma((STEPS, 2)),
            dma((STEPS, n)),
            dma((STEPS, n)),
        ],
        compiler_params=pltpu.CompilerParams(
            collective_id=0, has_side_effects=True, vmem_limit_bytes=56 * 1024 * 1024
        ),
    )(
        residual_input,
        jnp.broadcast_to(attention_norm_gain.astype(f32)[None, :], (rows, width)),
        request_adapter,
        cached_lengths,
        wq,
        wk,
        wv,
        wo,
        jnp.swapaxes(query_down_factor, 1, 2),
        query_up_factor,
        jnp.swapaxes(value_down_factor, 1, 2),
        value_up_factor,
        rotated_key_cache.reshape(ctx_dev * rows, hd),
        cached_value_rows.reshape(ctx_dev * rows, hd),
    )


def solution(mesh):
    n = mesh.shape["tensor"]
    body = functools.partial(fused, n) if n == 2 * KEY_VALUE_HEADS else local
    in_specs = (
        P("parts", "tensor"),
        P("tensor"),
        P("tensor", None),
        P("tensor", None),
        P("tensor", None),
        P("tensor", None),
        P(None, "tensor", None),
        P(None, None, "tensor"),
        P(None, "tensor", None),
        P(None, None, "tensor"),
        P("parts"),
        P("parts"),
        P("tensor", "parts", None),
        P("tensor", "parts", None),
    )
    out_specs = P(None, "parts", "tensor")
    return jax.shard_map(body, mesh=mesh, in_specs=in_specs, out_specs=out_specs, check_vma=False)
```

```python
import functools
import math

import jax
import jax.numpy as jnp
from jax import lax
from jax.experimental import pallas as pl
from jax.experimental.pallas import tpu as pltpu
from jax.sharding import PartitionSpec as P

MODEL_WIDTH = 8192
QUERY_HEADS = 64
KEY_VALUE_HEADS = 8
HEAD_DIMENSION = 128
STEPS = 2


theta_base = 500000.0
adapter_scale = 0.5
big_negative = -1e30
eps_norm = 1e-05


def merged(x, axis, combine):
    everything = jax.tree.map(
        lambda part, kind: lax.all_gather(part.astype(kind), axis),
        x,
        (jnp.bfloat16, jnp.bfloat16, jnp.bfloat16),
    )

    def take(k):
        return jax.tree.map(lambda part, own: part[k].astype(own.dtype), everything, x)

    return lax.fori_loop(
        1, lax.axis_size(axis), lambda k, so_far: combine(so_far, take(k)), take(0)
    )


def contract_final_axis(left, right):
    return lax.dot_general(
        left, right, (((1,), (1,)), ((), ())), preferred_element_type=jnp.float32
    )


def rotate_pairs(vectors, offset, positions):
    row_count, col_count = vectors.shape
    paired = vectors.reshape(row_count, col_count // 2, 2)
    pair_index = (offset // 2 + jnp.arange(col_count // 2, dtype=jnp.int32)) % (HEAD_DIMENSION // 2)
    frequency = jnp.power(
        jnp.float32(theta_base), -2.0 * pair_index.astype(jnp.float32) / HEAD_DIMENSION
    )
    angles = positions[:, None] * frequency[None, :]
    cosine = jnp.cos(angles)
    sine_part = jnp.sin(angles)
    even_part = paired[:, :, 0]
    odd_part = paired[:, :, 1]
    turned = jnp.stack(
        [even_part * cosine - odd_part * sine_part, even_part * sine_part + odd_part * cosine],
        axis=2,
    )
    return turned.reshape(row_count, col_count)


def adapter_down_project(normalized_input, adapter_indicator, factor):
    adapter_count, depth_rows, rank_size = factor.shape
    flat_table = jnp.transpose(factor, (1, 0, 2)).reshape(depth_rows, adapter_count * rank_size)
    spread = jnp.dot(normalized_input, flat_table, preferred_element_type=jnp.float32).reshape(
        -1, adapter_count, rank_size
    )
    return jnp.sum(spread * adapter_indicator.astype(jnp.float32)[:, :, None], axis=1)


def adapter_row_select(shrink_low, adapter_indicator, factor):
    spread = (adapter_indicator[:, :, None] * shrink_low[:, None, :]).reshape(
        shrink_low.shape[0], -1
    )
    return jnp.dot(spread, factor.reshape(-1, factor.shape[2]), preferred_element_type=jnp.float32)


def combine_parts(earlier, later):
    peak_one, total_one, summed_one = earlier
    peak_two, total_two, summed_two = later
    peak_both = jnp.maximum(peak_one, peak_two)
    scale_one = jnp.exp(peak_one - peak_both)
    scale_two = jnp.exp(peak_two - peak_both)
    row_count, head_count = peak_one.shape
    head_size = summed_one.shape[1] // head_count
    summed_both = summed_one.reshape(row_count, head_count, head_size) * scale_one[:, :, None]
    summed_both = (
        summed_both + summed_two.reshape(row_count, head_count, head_size) * scale_two[:, :, None]
    )
    return (
        peak_both,
        total_one * scale_one + total_two * scale_two,
        summed_both.reshape(row_count, head_count * head_size),
    )


def local(
    residual_input,
    attention_norm_gain,
    wq,
    wk,
    wv,
    wo,
    query_down_factor,
    query_up_factor,
    value_down_factor,
    value_up_factor,
    request_adapter,
    cached_lengths,
    rotated_key_cache,
    cached_value_rows,
):
    my_index = lax.axis_index("tensor")
    kv_group = my_index % KEY_VALUE_HEADS
    seq_block = my_index // KEY_VALUE_HEADS
    row_count, local_width = residual_input.shape
    ctx_dev = rotated_key_cache.shape[0]
    q_cols = wq.shape[0]
    kv_cols = wk.shape[0]
    per_group = QUERY_HEADS // KEY_VALUE_HEADS
    score_scale = HEAD_DIMENSION ** (-0.5)
    adapter_indicator = (
        request_adapter[:, None] == jnp.arange(query_down_factor.shape[0], dtype=jnp.int32)[None, :]
    ).astype(jnp.bfloat16)
    cache_pos = seq_block * ctx_dev + jnp.arange(ctx_dev, dtype=jnp.int32)
    cache_live = cache_pos[None, :] < cached_lengths[:, None]
    first_block = seq_block == 0
    group_mask = jnp.arange(KEY_VALUE_HEADS, dtype=jnp.int32) == kv_group
    group_float = group_mask.astype(jnp.float32)
    current = residual_input
    outputs = []
    fresh_keys = []
    fresh_values = []
    for step_index in range(STEPS):
        positions = (cached_lengths + step_index).astype(jnp.float32)
        widened = current.astype(jnp.float32)
        squares = lax.psum(jnp.sum(widened * widened, axis=1), "tensor")
        inv_rms = lax.rsqrt(squares / MODEL_WIDTH + eps_norm)
        local_normalized = (
            widened * inv_rms[:, None] * attention_norm_gain.astype(jnp.float32)[None, :]
        ).astype(jnp.bfloat16)
        part_rows = lax.all_gather(local_normalized, "tensor", axis=1, tiled=True)
        query_sum = contract_final_axis(part_rows, wq)
        k_sum = contract_final_axis(part_rows, wk)
        value_sum = contract_final_axis(part_rows, wv)
        query_down_output, value_down_output = lax.psum(
            (
                adapter_down_project(local_normalized, adapter_indicator, query_down_factor),
                adapter_down_project(local_normalized, adapter_indicator, value_down_factor),
            ),
            "tensor",
        )
        query_vector = query_sum + adapter_scale * adapter_row_select(
            query_down_output.astype(jnp.bfloat16), adapter_indicator, query_up_factor
        )
        query_vector = rotate_pairs(query_vector, my_index * q_cols, positions).astype(jnp.bfloat16)
        key_new = rotate_pairs(k_sum, my_index * kv_cols, positions).astype(jnp.bfloat16)
        value_current = (
            value_sum
            + adapter_scale
            * adapter_row_select(
                value_down_output.astype(jnp.bfloat16), adapter_indicator, value_up_factor
            )
        ).astype(jnp.bfloat16)
        full_q, full_k, full_v = (
            lax.all_gather(query_vector, "tensor", axis=1, tiled=True),
            lax.all_gather(key_new, "tensor", axis=1, tiled=True),
            lax.all_gather(value_current, "tensor", axis=1, tiled=True),
        )
        group_q = lax.dynamic_slice_in_dim(
            full_q, kv_group * per_group * HEAD_DIMENSION, per_group * HEAD_DIMENSION, 1
        ).reshape(row_count, per_group, HEAD_DIMENSION)
        fresh_keys.append(
            lax.dynamic_slice_in_dim(full_k, kv_group * HEAD_DIMENSION, HEAD_DIMENSION, 1)
        )
        fresh_values.append(
            lax.dynamic_slice_in_dim(full_v, kv_group * HEAD_DIMENSION, HEAD_DIMENSION, 1)
        )
        fresh_k = jnp.stack(fresh_keys, axis=1)
        fresh_v = jnp.stack(fresh_values, axis=1)
        cached = (
            jnp.einsum(
                "bgd,pbd->bgp", group_q, rotated_key_cache, preferred_element_type=jnp.float32
            )
            * score_scale
        )
        fresh_scores = (
            jnp.einsum("bgd,bsd->bgs", group_q, fresh_k, preferred_element_type=jnp.float32)
            * score_scale
        )
        cached = jnp.where(cache_live[:, None, :], cached, big_negative)
        fresh_scores = jnp.where(first_block, fresh_scores, big_negative)
        local_peak = jnp.maximum(jnp.max(cached, axis=2), jnp.max(fresh_scores, axis=2))
        cache_w = jnp.where(cache_live[:, None, :], jnp.exp(cached - local_peak[:, :, None]), 0.0)
        fresh_w = jnp.where(first_block, jnp.exp(fresh_scores - local_peak[:, :, None]), 0.0)
        local_total = jnp.sum(cache_w, axis=2) + jnp.sum(fresh_w, axis=2)
        weighted = jnp.einsum(
            "bgp,pbd->bgd",
            cache_w.astype(jnp.bfloat16),
            cached_value_rows,
            preferred_element_type=jnp.float32,
        )
        weighted = weighted + jnp.einsum(
            "bgs,bsd->bgd",
            fresh_w.astype(jnp.bfloat16),
            fresh_v,
            preferred_element_type=jnp.float32,
        )
        maxima = jnp.where(group_mask[None, :, None], local_peak[:, None, :], big_negative).reshape(
            row_count, QUERY_HEADS
        )
        totals = (group_float[None, :, None] * local_total[:, None, :]).reshape(
            row_count, QUERY_HEADS
        )
        values_all = (group_float[None, :, None, None] * weighted[:, None, :, :]).reshape(
            row_count, QUERY_HEADS * HEAD_DIMENSION
        )
        peak_all, denominator, summed = merged(
            (maxima, totals, values_all), "tensor", combine_parts
        )
        attention = (
            (summed.reshape(row_count, QUERY_HEADS, HEAD_DIMENSION) / denominator[:, :, None])
            .reshape(row_count, QUERY_HEADS * HEAD_DIMENSION)
            .astype(jnp.bfloat16)
        )
        projected = contract_final_axis(attention, wo)
        current = (widened + projected).astype(jnp.bfloat16)
        outputs.append(current)
    return jnp.stack(outputs, axis=0)


def fused_kernel(
    n,
    ctx_dev,
    current_ref,
    gain_ref,
    adapter_ref,
    length_ref,
    wq_hbm,
    wk_hbm,
    wv_hbm,
    wo_hbm,
    qd_hbm,
    qu_hbm,
    vd_hbm,
    vu_hbm,
    kc_hbm,
    vc_hbm,
    out_ref,
    w_s,
    wo_s,
    qd_s,
    vd_s,
    qu_s,
    vu_s,
    k_s,
    v_s,
    dq_s,
    dv_s,
    uq_s,
    uv_s,
    xg,
    sg,
    qg,
    og,
    xsend,
    ssend,
    qsend,
    osend,
    load_sem,
    x_send_sem,
    x_recv_sem,
    s_send_sem,
    s_recv_sem,
    q_send_sem,
    q_recv_sem,
    o_send_sem,
    o_recv_sem,
    o_pass_sem,
):
    f32, bf16 = jnp.float32, jnp.bfloat16
    hd, groups = HEAD_DIMENSION, KEY_VALUE_HEADS
    rows, width = current_ref.shape
    q_cols, kv_cols = wq_hbm.shape[0], wk_hbm.shape[0]
    chunks = width // hd
    heads_here = q_cols // hd
    per_group = QUERY_HEADS // groups
    blocks = n // groups
    span = 4
    cached_rows = ctx_dev * rows
    rank = qd_hbm.shape[1]
    me = lax.axis_index("tensor")

    loads = []

    def load(src, dst):
        copy = pltpu.make_async_copy(src, dst, load_sem.at[len(loads)])
        copy.start()
        loads.append(copy)
        return copy

    small = [
        load(qd_hbm, qd_s),
        load(vd_hbm, vd_s),
    ]
    pieces = 4
    step_cols = MODEL_WIDTH // pieces
    weights = []
    for piece in range(pieces):
        cols = pl.ds(piece * step_cols, step_cols)
        weights.append(
            [
                load(wq_hbm.at[:, cols], w_s.at[pl.ds(0, q_cols), cols]),
                load(wk_hbm.at[:, cols], w_s.at[pl.ds(q_cols, kv_cols), cols]),
                load(wv_hbm.at[:, cols], w_s.at[pl.ds(q_cols + kv_cols, kv_cols), cols]),
            ]
        )
    ups = [load(qu_hbm, qu_s), load(vu_hbm, vu_s)]
    caches = [
        load(kc_hbm, k_s.at[pl.ds(0, cached_rows)]),
        load(vc_hbm, v_s.at[pl.ds(0, cached_rows)]),
    ]
    out_weights = []
    for piece in range(pieces):
        cols = pl.ds(piece * step_cols, step_cols)
        out_weights.append(load(wo_hbm.at[:, cols], wo_s.at[:, cols]))

    barrier = pltpu.get_barrier_semaphore()

    def greet(k, carry):
        pl.semaphore_signal(
            barrier,
            inc=1,
            device_id={"tensor": lax.rem(me + k, n)},
            device_id_type=pl.DeviceIdType.MESH,
        )
        return carry

    lax.fori_loop(1, n, greet, 0)

    def remote(src, dst, send_sem, recv_sem, target):
        return pltpu.make_async_remote_copy(
            src_ref=src,
            dst_ref=dst,
            send_sem=send_sem,
            recv_sem=recv_sem,
            device_id={"tensor": target},
            device_id_type=pl.DeviceIdType.MESH,
        )

    def for_others(body):
        def step(k, carry):
            body(lax.rem(me + k, n))
            return carry

        lax.fori_loop(1, n, step, 0)

    def x_copy(t, slot, target):
        return remote(
            xsend.at[t], xg.at[t, slot], x_send_sem.at[t, target], x_recv_sem.at[t, slot], target
        )

    def s_copy(t, slot, target):
        return remote(
            ssend.at[t], sg.at[t, slot], s_send_sem.at[t, target], s_recv_sem.at[t, slot], target
        )

    def o_copy(t, slot, target):
        return remote(
            osend.at[t], og.at[t, slot], o_send_sem.at[t, target], o_recv_sem.at[t, slot], target
        )

    def o_pass(t, slot, target):
        return remote(
            og.at[t, slot], og.at[t, slot], o_pass_sem.at[t, slot], o_recv_sem.at[t, slot], target
        )

    def q_copy(t, slot, block, target):
        return remote(
            qsend.at[t], qg.at[t, slot], q_send_sem.at[t, block], q_recv_sem.at[t, slot], target
        )

    lane = lax.broadcasted_iota(jnp.int32, (rows, hd), 1)
    row = lax.broadcasted_iota(jnp.int32, (rows, hd), 0)
    gains = gain_ref[...]

    def split_chunks(x):
        return [x[:, c * hd : (c + 1) * hd] for c in range(x.shape[1] // hd)]

    current = current_ref[...].astype(f32)
    def send_state(t):
        message = jnp.concatenate(split_chunks(current * gains), axis=0).astype(bf16)
        xsend[t] = message
        xg[t, me] = message
        if t == 0:
            pl.semaphore_wait(barrier, n - 1)
        for_others(lambda target: x_copy(t, me, target).start())

    send_state(0)

    lengths = jnp.zeros((rows, hd), jnp.int32)
    for r in range(rows):
        lengths = jnp.where(row == r, length_ref[r], lengths)
    lane_even = lax.rem(lane, 2) == 0

    def angle_tables(pair, positions):
        frequency = jnp.exp(pair.astype(f32) * jnp.float32(-2.0 * math.log(theta_base) / hd))
        angles = positions * frequency
        sine = jnp.sin(angles)
        return jnp.cos(angles), jnp.where(lane_even, -sine, sine)

    fresh_pair = lax.rem(me, 2) * (kv_cols // 2) + lax.rem(lane, kv_cols) // 2
    is_key = lane < kv_cols
    tables = []
    for t in range(STEPS):
        positions = (lengths + t).astype(f32)
        q_cos, q_sin = angle_tables(lane // 2, positions)
        k_cos, k_sin = angle_tables(fresh_pair, positions)
        tables.append(
            (q_cos, q_sin, jnp.where(is_key, k_cos, 1.0), jnp.where(is_key, k_sin, 0.0))
        )

    def rotate(x, cosine, sine):
        swapped = jnp.where(lane_even, pltpu.roll(x, hd - 1, 1), pltpu.roll(x, 1, 1))
        return x * cosine + swapped * sine

    extra = k_s.shape[0] - cached_rows
    k_s[pl.ds(cached_rows, extra)] = jnp.zeros((extra, hd), bf16)
    v_s[pl.ds(cached_rows, extra)] = jnp.zeros((extra, hd), bf16)

    column = lax.broadcasted_iota(jnp.int32, (rows, cached_rows + extra), 1)
    wide_row = lax.broadcasted_iota(jnp.int32, (rows, cached_rows + extra), 0)
    seq_block = me // groups
    wide_length = jnp.zeros((rows, cached_rows + extra), jnp.int32)
    for r in range(rows):
        wide_length = jnp.where(wide_row == r, length_ref[r], wide_length)
    own_cached = (
        (column < cached_rows)
        & (lax.rem(column, rows) == wide_row)
        & (seq_block * ctx_dev + column // rows < wide_length)
    )
    fresh_column = column - cached_rows
    fresh_row = (fresh_column >= 0) & (lax.rem(column, 16) == wide_row) & (seq_block == 0)

    for copy in small:
        copy.wait()
    for r in range(rows):
        adapter = adapter_ref[r]
        dq_s[pl.ds(r * rank, rank)] = qd_s[adapter]
        dv_s[pl.ds(r * rank, rank)] = vd_s[adapter]

    spread_column = lax.broadcasted_iota(jnp.int32, (rows, rows * rank), 1)
    spread_row = lax.broadcasted_iota(jnp.int32, (rows, rows * rank), 0)
    own_block = spread_column // rank == spread_row
    lane_block = lane // rank

    def flip(index, bits):
        bit = 1
        while bit <= bits:
            if bits & bit:
                index = index + bit - 2 * bit * lax.rem(index // bit, 2)
            bit *= 2
        return index

    def contract(left, right):
        return lax.dot_general(
            left, right, (((1,), (1,)), ((), ())), preferred_element_type=f32
        )

    def fold(x):
        x = jnp.where(own_block, x, 0.0)
        parts = split_chunks(x)
        total = parts[0]
        for part in parts[1:]:
            total = total + part
        shift = hd // 2
        while shift >= rank:
            total = total + pltpu.roll(total, shift, 1)
            shift //= 2
        return total

    def send_shrink(t):
        scaled = (current * gains).astype(bf16)
        squares = jnp.sum(current * current, axis=1, keepdims=True)
        both = jnp.where(
            lane_block == 0,
            fold(contract(scaled, dq_s[...])),
            jnp.where(lane_block == 1, fold(contract(scaled, dv_s[...])), squares),
        )
        ssend[t] = both
        sg[t, me] = both
        for_others(lambda target: s_copy(t, me, target).start())

    send_shrink(0)

    for t in range(STEPS):
        if t == 0:
            for copies in weights:
                for copy in copies:
                    copy.wait()
        products = jnp.zeros((rows, q_cols + 2 * kv_cols), f32)
        for far in range(0, n, span):
            first = flip(me, far) // span * span
            parts = []
            for k in range(span):
                source = first + k
                if far:
                    x_copy(t, source, source).wait_recv()
                else:

                    @pl.when(source != me)
                    def _():
                        x_copy(t, source, source).wait_recv()

                block = xg[t, source].astype(f32)
                parts += [block[c * rows : (c + 1) * rows] for c in range(chunks)]
            cols = pl.ds(pl.multiple_of(first * width, span * width), span * width)
            state = jnp.concatenate(parts, axis=1).astype(bf16)
            products = products + contract(state, w_s[:, cols])
        if t == 0:
            for copy in ups:
                copy.wait()
            for r in range(rows):
                adapter = adapter_ref[r]
                uq_s[pl.ds(r * rank, rank)] = qu_s[adapter]
                uv_s[pl.ds(r * rank, rank)] = vu_s[adapter]
        for_others(lambda source: s_copy(t, source, source).wait_recv())
        shrink = sg[t, 0]
        for d in range(1, n):
            shrink = shrink + sg[t, d]
        squares = shrink[:, 2 * rank : 2 * rank + 1]
        inv_rms = lax.rsqrt(squares / MODEL_WIDTH + eps_norm)
        shrink = shrink * inv_rms

        def spread(kind):
            x = jnp.where(lane_block == kind, shrink, 0.0)
            shift = rank
            while shift < hd:
                x = x + pltpu.roll(x, shift, 1)
                shift *= 2
            x = jnp.concatenate([x] * (rows * rank // hd), axis=1)
            return jnp.where(own_block, x, 0.0).astype(bf16)

        q_low = spread(0)
        v_low = spread(1)
        products = products * inv_rms
        q_up = jnp.dot(q_low, uq_s[...], preferred_element_type=f32)
        v_up = jnp.dot(v_low, uv_s[...], preferred_element_type=f32)
        query = products[:, :q_cols] + adapter_scale * q_up
        fresh = products[:, q_cols:] + adapter_scale * jnp.concatenate(
            [jnp.zeros((rows, kv_cols), f32), v_up], axis=1
        )
        q_cos, q_sin, k_cos, k_sin = tables[t]
        parts = [rotate(part, q_cos, q_sin) for part in split_chunks(query)]
        parts.append(rotate(fresh, k_cos, k_sin))
        parts.append(jnp.zeros((rows, hd), f32))
        message = jnp.concatenate(parts, axis=0).astype(bf16)
        qsend[t] = message
        side = lax.rem(me, 2)
        for block in range(blocks):
            target = me // 2 + block * groups

            @pl.when(target == me)
            def _():
                qg[t, side] = message

            @pl.when(target != me)
            def _():
                q_copy(t, side, block, target).start()

        if t == 0:
            for copy in caches:
                copy.wait()
        for half in range(2):
            source = 2 * lax.rem(me, groups) + half

            @pl.when(source != me)
            def _():
                q_copy(t, half, 0, source).wait_recv()

        first = qg[t, 0].astype(f32)
        second = qg[t, 1].astype(f32)
        q_rows = heads_here * rows
        queries = jnp.concatenate([first[:q_rows], second[:q_rows]], axis=0).astype(bf16)
        first_kv = first[q_rows : q_rows + rows]
        second_kv = second[q_rows : q_rows + rows]
        key_new = jnp.where(is_key, first_kv, pltpu.roll(second_kv, kv_cols, 1))
        value_new = jnp.where(is_key, pltpu.roll(first_kv, kv_cols, 1), second_kv)
        blank = jnp.zeros((16 - rows, hd), f32)
        k_s[pl.ds(cached_rows + 16 * t, 16)] = jnp.concatenate([key_new, blank], 0).astype(bf16)
        v_s[pl.ds(cached_rows + 16 * t, 16)] = jnp.concatenate([value_new, blank], 0).astype(bf16)
        scores = contract(queries, k_s[...]) * (HEAD_DIMENSION ** (-0.5))
        scores = scores.reshape(per_group, rows, cached_rows + extra)
        live = (own_cached | (fresh_row & (fresh_column < 16 * (t + 1))))[None]
        scores = jnp.where(live, scores, big_negative)
        peak = jnp.max(scores, axis=2, keepdims=True)
        weight = jnp.where(live, jnp.exp(scores - peak), 0.0)
        mass = jnp.sum(weight, axis=2, keepdims=True)
        weight = weight.reshape(per_group * rows, cached_rows + extra).astype(bf16)
        summed = jnp.dot(weight, v_s[...], preferred_element_type=f32)
        summed = summed.reshape(per_group, rows, hd)
        some = mass > 0.0
        safe = jnp.where(some, mass, 1.0)
        partial = summed / safe
        level = jnp.where(some, peak + jnp.log(safe), big_negative)
        levels = jnp.zeros((rows, hd), f32)
        for h in range(per_group):
            levels = jnp.where(lane == h, level[h], levels)
        high = levels.astype(bf16).astype(f32)
        middle = (levels - high).astype(bf16).astype(f32)
        low = levels - high - middle
        packed = high + pltpu.roll(middle, per_group, 1) + pltpu.roll(low, 2 * per_group, 1)
        message = jnp.concatenate(
            [partial.reshape(per_group * rows, hd), packed, jnp.zeros((16 - rows, hd), f32)], axis=0
        ).astype(bf16)
        osend[t] = message
        og[t, me] = message
        for k in range(2, n, 2):
            o_copy(t, me, flip(me, k)).start()
        sibling = flip(me, 1)
        o_copy(t, me, sibling).start()
        if t == 0:
            for copy in out_weights:
                copy.wait()
        projected = jnp.zeros((rows, width), f32)
        own_group = lax.rem(me, groups)
        order = [k for k in range(groups) if k % 2 == 0] + [k for k in range(groups) if k % 2]
        for k in order:
            g = flip(own_group, k)
            found = []
            for b in range(blocks):
                source = b * groups + g
                if k % 2:
                    o_copy(t, source, source).wait_recv()
                elif k:
                    o_copy(t, source, source).wait_recv()
                    o_pass(t, source, sibling).start()
                else:

                    @pl.when(source != me)
                    def _():
                        o_copy(t, source, source).wait_recv()
                        o_pass(t, source, sibling).start()

            for b in range(blocks):
                entry = og[t, b * groups + g].astype(f32)
                packed = entry[per_group * rows : per_group * rows + rows]
                level = (
                    packed
                    + pltpu.roll(packed, hd - per_group, 1)
                    + pltpu.roll(packed, hd - 2 * per_group, 1)
                )
                found.append((level, entry))
            top = found[0][0]
            for level, _ in found[1:]:
                top = jnp.maximum(top, level)
            shares = [jnp.exp(level - top) for level, _ in found]
            whole = shares[0]
            for share in shares[1:]:
                whole = whole + share
            shares = [share / whole for share in shares]
            parts = []
            for h in range(per_group):
                value = jnp.zeros((rows, hd), f32)
                for share, (_, entry) in zip(shares, found):
                    value = value + share[:, h : h + 1] * entry[h * rows : (h + 1) * rows]
                parts.append(value)
            attention = jnp.concatenate(parts, axis=1).astype(bf16)
            wide = per_group * hd
            cols = pl.ds(pl.multiple_of(g * wide, wide), wide)
            projected = projected + contract(attention, wo_s[:, cols])
        rounded = (current + projected).astype(bf16)
        out_ref[t] = rounded
        current = rounded.astype(f32)
        if t + 1 < STEPS:
            send_state(t + 1)
            send_shrink(t + 1)

    for t in range(STEPS):
        for_others(lambda target: x_copy(t, me, target).wait_send())
        for_others(lambda target: s_copy(t, me, target).wait_send())
        for k in range(2, n, 2):
            other = flip(me, k)
            o_copy(t, me, other).wait_send()
            o_pass(t, other, flip(me, 1)).wait_send()
        o_copy(t, me, flip(me, 1)).wait_send()
        for block in range(blocks):
            target = me // 2 + block * groups

            @pl.when(target != me)
            def _():
                q_copy(t, 0, block, target).wait_send()


def fused(
    n,
    residual_input,
    attention_norm_gain,
    wq,
    wk,
    wv,
    wo,
    query_down_factor,
    query_up_factor,
    value_down_factor,
    value_up_factor,
    request_adapter,
    cached_lengths,
    rotated_key_cache,
    cached_value_rows,
):
    rows, width = residual_input.shape
    ctx_dev = rotated_key_cache.shape[0]
    q_cols, kv_cols = wq.shape[0], wk.shape[0]
    adapters, _, rank = query_down_factor.shape
    hd = HEAD_DIMENSION
    chunks = width // hd
    per_group = QUERY_HEADS // KEY_VALUE_HEADS
    blocks = n // KEY_VALUE_HEADS
    kv_rows = ctx_dev * rows + 128
    x_rows = chunks * rows
    q_rows = (q_cols // hd + 2) * rows
    o_rows = per_group * rows + 16
    bf16, f32 = jnp.bfloat16, jnp.float32
    dma = pltpu.SemaphoreType.DMA
    any_spec = pl.BlockSpec(memory_space=pl.ANY)
    vmem = pl.BlockSpec(memory_space=pltpu.VMEM)
    smem = pl.BlockSpec(memory_space=pltpu.SMEM)
    return pl.pallas_call(
        functools.partial(fused_kernel, n, ctx_dev),
        out_shape=jax.ShapeDtypeStruct((STEPS, rows, width), bf16),
        in_specs=[vmem, vmem, smem, smem] + [any_spec] * 10,
        out_specs=vmem,
        scratch_shapes=[
            pltpu.VMEM((q_cols + 2 * kv_cols, MODEL_WIDTH), bf16),
            pltpu.VMEM((width, MODEL_WIDTH), bf16),
            pltpu.VMEM((adapters, rank, width), bf16),
            pltpu.VMEM((adapters, rank, width), bf16),
            pltpu.VMEM((adapters, rank, q_cols), bf16),
            pltpu.VMEM((adapters, rank, kv_cols), bf16),
            pltpu.VMEM((kv_rows, hd), bf16),
            pltpu.VMEM((kv_rows, hd), bf16),
            pltpu.VMEM((rows * rank, width), bf16),
            pltpu.VMEM((rows * rank, width), bf16),
            pltpu.VMEM((rows * rank, q_cols), bf16),
            pltpu.VMEM((rows * rank, kv_cols), bf16),
            pltpu.VMEM((STEPS, n, x_rows, hd), bf16),
            pltpu.VMEM((STEPS, n, rows, hd), f32),
            pltpu.VMEM((STEPS, 2, q_rows, hd), bf16),
            pltpu.VMEM((STEPS, n, o_rows, hd), bf16),
            pltpu.VMEM((STEPS, x_rows, hd), bf16),
            pltpu.VMEM((STEPS, rows, hd), f32),
            pltpu.VMEM((STEPS, q_rows, hd), bf16),
            pltpu.VMEM((STEPS, o_rows, hd), bf16),
            dma((24,)),
            dma((STEPS, n)),
            dma((STEPS, n)),
            dma((STEPS, n)),
            dma((STEPS, n)),
            dma((STEPS, blocks)),
            dma((STEPS, 2)),
            dma((STEPS, n)),
            dma((STEPS, n)),
            dma((STEPS, n)),
        ],
        compiler_params=pltpu.CompilerParams(
            collective_id=0, has_side_effects=True, vmem_limit_bytes=56 * 1024 * 1024
        ),
    )(
        residual_input,
        jnp.broadcast_to(attention_norm_gain.astype(f32)[None, :], (rows, width)),
        request_adapter,
        cached_lengths,
        wq,
        wk,
        wv,
        wo,
        jnp.swapaxes(query_down_factor, 1, 2),
        query_up_factor,
        jnp.swapaxes(value_down_factor, 1, 2),
        value_up_factor,
        rotated_key_cache.reshape(ctx_dev * rows, hd),
        cached_value_rows.reshape(ctx_dev * rows, hd),
    )


def solution(mesh):
    n = mesh.shape["tensor"]
    body = functools.partial(fused, n) if n == 2 * KEY_VALUE_HEADS else local
    in_specs = (
        P("parts", "tensor"),
        P("tensor"),
        P("tensor", None),
        P("tensor", None),
        P("tensor", None),
        P("tensor", None),
        P(None, "tensor", None),
        P(None, None, "tensor"),
        P(None, "tensor", None),
        P(None, None, "tensor"),
        P("parts"),
        P("parts"),
        P("tensor", "parts", None),
        P("tensor", "parts", None),
    )
    out_specs = P(None, "parts", "tensor")
    return jax.shard_map(body, mesh=mesh, in_specs=in_specs, out_specs=out_specs, check_vma=False)
```

```python
import functools
import math

import jax
import jax.numpy as jnp
from jax import lax
from jax.experimental import pallas as pl
from jax.experimental.pallas import tpu as pltpu
from jax.sharding import PartitionSpec as P

MODEL_WIDTH = 8192
QUERY_HEADS = 64
KEY_VALUE_HEADS = 8
HEAD_DIMENSION = 128
STEPS = 2


theta_base = 500000.0
adapter_scale = 0.5
big_negative = -1e30
eps_norm = 1e-05


def merged(x, axis, combine):
    everything = jax.tree.map(
        lambda part, kind: lax.all_gather(part.astype(kind), axis),
        x,
        (jnp.bfloat16, jnp.bfloat16, jnp.bfloat16),
    )

    def take(k):
        return jax.tree.map(lambda part, own: part[k].astype(own.dtype), everything, x)

    return lax.fori_loop(
        1, lax.axis_size(axis), lambda k, so_far: combine(so_far, take(k)), take(0)
    )


def contract_final_axis(left, right):
    return lax.dot_general(
        left, right, (((1,), (1,)), ((), ())), preferred_element_type=jnp.float32
    )


def rotate_pairs(vectors, offset, positions):
    row_count, col_count = vectors.shape
    paired = vectors.reshape(row_count, col_count // 2, 2)
    pair_index = (offset // 2 + jnp.arange(col_count // 2, dtype=jnp.int32)) % (HEAD_DIMENSION // 2)
    frequency = jnp.power(
        jnp.float32(theta_base), -2.0 * pair_index.astype(jnp.float32) / HEAD_DIMENSION
    )
    angles = positions[:, None] * frequency[None, :]
    cosine = jnp.cos(angles)
    sine_part = jnp.sin(angles)
    even_part = paired[:, :, 0]
    odd_part = paired[:, :, 1]
    turned = jnp.stack(
        [even_part * cosine - odd_part * sine_part, even_part * sine_part + odd_part * cosine],
        axis=2,
    )
    return turned.reshape(row_count, col_count)


def adapter_down_project(normalized_input, adapter_indicator, factor):
    adapter_count, depth_rows, rank_size = factor.shape
    flat_table = jnp.transpose(factor, (1, 0, 2)).reshape(depth_rows, adapter_count * rank_size)
    spread = jnp.dot(normalized_input, flat_table, preferred_element_type=jnp.float32).reshape(
        -1, adapter_count, rank_size
    )
    return jnp.sum(spread * adapter_indicator.astype(jnp.float32)[:, :, None], axis=1)


def adapter_row_select(shrink_low, adapter_indicator, factor):
    spread = (adapter_indicator[:, :, None] * shrink_low[:, None, :]).reshape(
        shrink_low.shape[0], -1
    )
    return jnp.dot(spread, factor.reshape(-1, factor.shape[2]), preferred_element_type=jnp.float32)


def combine_parts(earlier, later):
    peak_one, total_one, summed_one = earlier
    peak_two, total_two, summed_two = later
    peak_both = jnp.maximum(peak_one, peak_two)
    scale_one = jnp.exp(peak_one - peak_both)
    scale_two = jnp.exp(peak_two - peak_both)
    row_count, head_count = peak_one.shape
    head_size = summed_one.shape[1] // head_count
    summed_both = summed_one.reshape(row_count, head_count, head_size) * scale_one[:, :, None]
    summed_both = (
        summed_both + summed_two.reshape(row_count, head_count, head_size) * scale_two[:, :, None]
    )
    return (
        peak_both,
        total_one * scale_one + total_two * scale_two,
        summed_both.reshape(row_count, head_count * head_size),
    )


def local(
    residual_input,
    attention_norm_gain,
    wq,
    wk,
    wv,
    wo,
    query_down_factor,
    query_up_factor,
    value_down_factor,
    value_up_factor,
    request_adapter,
    cached_lengths,
    rotated_key_cache,
    cached_value_rows,
):
    my_index = lax.axis_index("tensor")
    kv_group = my_index % KEY_VALUE_HEADS
    seq_block = my_index // KEY_VALUE_HEADS
    row_count, local_width = residual_input.shape
    ctx_dev = rotated_key_cache.shape[0]
    q_cols = wq.shape[0]
    kv_cols = wk.shape[0]
    per_group = QUERY_HEADS // KEY_VALUE_HEADS
    score_scale = HEAD_DIMENSION ** (-0.5)
    adapter_indicator = (
        request_adapter[:, None] == jnp.arange(query_down_factor.shape[0], dtype=jnp.int32)[None, :]
    ).astype(jnp.bfloat16)
    cache_pos = seq_block * ctx_dev + jnp.arange(ctx_dev, dtype=jnp.int32)
    cache_live = cache_pos[None, :] < cached_lengths[:, None]
    first_block = seq_block == 0
    group_mask = jnp.arange(KEY_VALUE_HEADS, dtype=jnp.int32) == kv_group
    group_float = group_mask.astype(jnp.float32)
    current = residual_input
    outputs = []
    fresh_keys = []
    fresh_values = []
    for step_index in range(STEPS):
        positions = (cached_lengths + step_index).astype(jnp.float32)
        widened = current.astype(jnp.float32)
        squares = lax.psum(jnp.sum(widened * widened, axis=1), "tensor")
        inv_rms = lax.rsqrt(squares / MODEL_WIDTH + eps_norm)
        local_normalized = (
            widened * inv_rms[:, None] * attention_norm_gain.astype(jnp.float32)[None, :]
        ).astype(jnp.bfloat16)
        part_rows = lax.all_gather(local_normalized, "tensor", axis=1, tiled=True)
        query_sum = contract_final_axis(part_rows, wq)
        k_sum = contract_final_axis(part_rows, wk)
        value_sum = contract_final_axis(part_rows, wv)
        query_down_output, value_down_output = lax.psum(
            (
                adapter_down_project(local_normalized, adapter_indicator, query_down_factor),
                adapter_down_project(local_normalized, adapter_indicator, value_down_factor),
            ),
            "tensor",
        )
        query_vector = query_sum + adapter_scale * adapter_row_select(
            query_down_output.astype(jnp.bfloat16), adapter_indicator, query_up_factor
        )
        query_vector = rotate_pairs(query_vector, my_index * q_cols, positions).astype(jnp.bfloat16)
        key_new = rotate_pairs(k_sum, my_index * kv_cols, positions).astype(jnp.bfloat16)
        value_current = (
            value_sum
            + adapter_scale
            * adapter_row_select(
                value_down_output.astype(jnp.bfloat16), adapter_indicator, value_up_factor
            )
        ).astype(jnp.bfloat16)
        full_q, full_k, full_v = (
            lax.all_gather(query_vector, "tensor", axis=1, tiled=True),
            lax.all_gather(key_new, "tensor", axis=1, tiled=True),
            lax.all_gather(value_current, "tensor", axis=1, tiled=True),
        )
        group_q = lax.dynamic_slice_in_dim(
            full_q, kv_group * per_group * HEAD_DIMENSION, per_group * HEAD_DIMENSION, 1
        ).reshape(row_count, per_group, HEAD_DIMENSION)
        fresh_keys.append(
            lax.dynamic_slice_in_dim(full_k, kv_group * HEAD_DIMENSION, HEAD_DIMENSION, 1)
        )
        fresh_values.append(
            lax.dynamic_slice_in_dim(full_v, kv_group * HEAD_DIMENSION, HEAD_DIMENSION, 1)
        )
        fresh_k = jnp.stack(fresh_keys, axis=1)
        fresh_v = jnp.stack(fresh_values, axis=1)
        cached = (
            jnp.einsum(
                "bgd,pbd->bgp", group_q, rotated_key_cache, preferred_element_type=jnp.float32
            )
            * score_scale
        )
        fresh_scores = (
            jnp.einsum("bgd,bsd->bgs", group_q, fresh_k, preferred_element_type=jnp.float32)
            * score_scale
        )
        cached = jnp.where(cache_live[:, None, :], cached, big_negative)
        fresh_scores = jnp.where(first_block, fresh_scores, big_negative)
        local_peak = jnp.maximum(jnp.max(cached, axis=2), jnp.max(fresh_scores, axis=2))
        cache_w = jnp.where(cache_live[:, None, :], jnp.exp(cached - local_peak[:, :, None]), 0.0)
        fresh_w = jnp.where(first_block, jnp.exp(fresh_scores - local_peak[:, :, None]), 0.0)
        local_total = jnp.sum(cache_w, axis=2) + jnp.sum(fresh_w, axis=2)
        weighted = jnp.einsum(
            "bgp,pbd->bgd",
            cache_w.astype(jnp.bfloat16),
            cached_value_rows,
            preferred_element_type=jnp.float32,
        )
        weighted = weighted + jnp.einsum(
            "bgs,bsd->bgd",
            fresh_w.astype(jnp.bfloat16),
            fresh_v,
            preferred_element_type=jnp.float32,
        )
        maxima = jnp.where(group_mask[None, :, None], local_peak[:, None, :], big_negative).reshape(
            row_count, QUERY_HEADS
        )
        totals = (group_float[None, :, None] * local_total[:, None, :]).reshape(
            row_count, QUERY_HEADS
        )
        values_all = (group_float[None, :, None, None] * weighted[:, None, :, :]).reshape(
            row_count, QUERY_HEADS * HEAD_DIMENSION
        )
        peak_all, denominator, summed = merged(
            (maxima, totals, values_all), "tensor", combine_parts
        )
        attention = (
            (summed.reshape(row_count, QUERY_HEADS, HEAD_DIMENSION) / denominator[:, :, None])
            .reshape(row_count, QUERY_HEADS * HEAD_DIMENSION)
            .astype(jnp.bfloat16)
        )
        projected = contract_final_axis(attention, wo)
        current = (widened + projected).astype(jnp.bfloat16)
        outputs.append(current)
    return jnp.stack(outputs, axis=0)


def fused_kernel(
    n,
    ctx_dev,
    current_ref,
    gain_ref,
    adapter_ref,
    length_ref,
    wq_hbm,
    wk_hbm,
    wv_hbm,
    wo_hbm,
    qd_hbm,
    qu_hbm,
    vd_hbm,
    vu_hbm,
    kc_hbm,
    vc_hbm,
    out_ref,
    w_s,
    wo_s,
    qd_s,
    vd_s,
    qu_s,
    vu_s,
    k_s,
    v_s,
    dq_s,
    dv_s,
    uq_s,
    uv_s,
    xg,
    sg,
    sp,
    qg,
    og,
    xsend,
    ssend,
    ssum,
    qsend,
    osend,
    load_sem,
    x_send_sem,
    x_recv_sem,
    x_pass_sem,
    s_send_sem,
    s_recv_sem,
    s_pair_sem,
    q_send_sem,
    q_recv_sem,
    o_send_sem,
    o_recv_sem,
    o_pass_sem,
):
    f32, bf16 = jnp.float32, jnp.bfloat16
    hd, groups = HEAD_DIMENSION, KEY_VALUE_HEADS
    rows, width = current_ref.shape
    q_cols, kv_cols = wq_hbm.shape[0], wk_hbm.shape[0]
    chunks = width // hd
    heads_here = q_cols // hd
    per_group = QUERY_HEADS // groups
    blocks = n // groups
    cached_rows = ctx_dev * rows
    rank = qd_hbm.shape[1]
    me = lax.axis_index("tensor")

    loads = []

    def load(src, dst):
        copy = pltpu.make_async_copy(src, dst, load_sem.at[len(loads)])
        copy.start()
        loads.append(copy)
        return copy

    small = [
        load(qd_hbm, qd_s),
        load(vd_hbm, vd_s),
    ]
    pieces = 4
    step_cols = MODEL_WIDTH // pieces
    weights = []
    for piece in range(pieces):
        cols = pl.ds(piece * step_cols, step_cols)
        weights.append(
            [
                load(wq_hbm.at[:, cols], w_s.at[pl.ds(0, q_cols), cols]),
                load(wk_hbm.at[:, cols], w_s.at[pl.ds(q_cols, kv_cols), cols]),
                load(wv_hbm.at[:, cols], w_s.at[pl.ds(q_cols + kv_cols, kv_cols), cols]),
            ]
        )
    ups = [load(qu_hbm, qu_s), load(vu_hbm, vu_s)]
    caches = [
        load(kc_hbm, k_s.at[pl.ds(0, cached_rows)]),
        load(vc_hbm, v_s.at[pl.ds(0, cached_rows)]),
    ]
    out_weights = []
    for piece in range(pieces):
        cols = pl.ds(piece * step_cols, step_cols)
        out_weights.append(load(wo_hbm.at[:, cols], wo_s.at[:, cols]))

    barrier = pltpu.get_barrier_semaphore()

    def greet(k, carry):
        pl.semaphore_signal(
            barrier,
            inc=1,
            device_id={"tensor": lax.rem(me + k, n)},
            device_id_type=pl.DeviceIdType.MESH,
        )
        return carry

    lax.fori_loop(1, n, greet, 0)

    def remote(src, dst, send_sem, recv_sem, target):
        return pltpu.make_async_remote_copy(
            src_ref=src,
            dst_ref=dst,
            send_sem=send_sem,
            recv_sem=recv_sem,
            device_id={"tensor": target},
            device_id_type=pl.DeviceIdType.MESH,
        )

    def x_copy(t, slot, target):
        return remote(
            xsend.at[t], xg.at[t, slot], x_send_sem.at[t, target], x_recv_sem.at[t, slot], target
        )

    def x_pass(t, slot, target):
        return remote(
            xg.at[t, slot], xg.at[t, slot], x_pass_sem.at[t, slot], x_recv_sem.at[t, slot], target
        )

    def s_pair(t):
        return remote(ssend.at[t], sp.at[t], s_pair_sem.at[t, 0], s_pair_sem.at[t, 1], sibling)

    def s_copy(t, slot, target):
        return remote(
            ssum.at[t],
            sg.at[t, slot // 2],
            s_send_sem.at[t, target // 2],
            s_recv_sem.at[t, slot // 2],
            target,
        )

    def o_copy(t, slot, target):
        return remote(
            osend.at[t], og.at[t, slot], o_send_sem.at[t, target], o_recv_sem.at[t, slot], target
        )

    def o_pass(t, slot, target):
        return remote(
            og.at[t, slot], og.at[t, slot], o_pass_sem.at[t, slot], o_recv_sem.at[t, slot], target
        )

    def q_copy(t, slot, block, target):
        return remote(
            qsend.at[t], qg.at[t, slot], q_send_sem.at[t, block], q_recv_sem.at[t, slot], target
        )

    def flip(index, bits):
        bit = 1
        while bit <= bits:
            if bits & bit:
                index = index + bit - 2 * bit * lax.rem(index // bit, 2)
            bit *= 2
        return index

    sibling = flip(me, 1)
    lane = lax.broadcasted_iota(jnp.int32, (rows, hd), 1)
    row = lax.broadcasted_iota(jnp.int32, (rows, hd), 0)
    gains = jnp.broadcast_to(gain_ref[...].astype(f32)[None, :], (rows, width))

    def split_chunks(x):
        return [x[:, c * hd : (c + 1) * hd] for c in range(x.shape[1] // hd)]

    current = current_ref[...].astype(f32)
    def send_state(t):
        message = jnp.concatenate(split_chunks(current * gains), axis=0).astype(bf16)
        xsend[t] = message
        xg[t, me] = message
        if t == 0:
            pl.semaphore_wait(barrier, n - 1)
        for k in (*range(2, n, 2), 1):
            x_copy(t, me, flip(me, k)).start()

    send_state(0)

    lengths = jnp.zeros((rows, hd), jnp.int32)
    for r in range(rows):
        lengths = jnp.where(row == r, length_ref[r], lengths)
    lane_even = (lane & 1) == 0

    def angle_tables(pair, positions):
        frequency = jnp.exp(pair.astype(f32) * jnp.float32(-2.0 * math.log(theta_base) / hd))
        angles = positions * frequency
        sine = jnp.sin(angles)
        return jnp.cos(angles), jnp.where(lane_even, -sine, sine)

    fresh_pair = lax.rem(me, 2) * (kv_cols // 2) + (lane & (kv_cols - 1)) // 2
    is_key = lane < kv_cols
    tables = []
    for t in range(STEPS):
        positions = (lengths + t).astype(f32)
        q_cos, q_sin = angle_tables(lane // 2, positions)
        k_cos, k_sin = angle_tables(fresh_pair, positions)
        tables.append(
            (q_cos, q_sin, jnp.where(is_key, k_cos, 1.0), jnp.where(is_key, k_sin, 0.0))
        )

    def rotate(x, cosine, sine):
        swapped = jnp.where(lane_even, pltpu.roll(x, hd - 1, 1), pltpu.roll(x, 1, 1))
        return x * cosine + swapped * sine

    extra = k_s.shape[0] - cached_rows
    k_s[pl.ds(cached_rows, extra)] = jnp.zeros((extra, hd), bf16)
    v_s[pl.ds(cached_rows, extra)] = jnp.zeros((extra, hd), bf16)

    column = lax.broadcasted_iota(jnp.int32, (rows, cached_rows + extra), 1)
    wide_row = lax.broadcasted_iota(jnp.int32, (rows, cached_rows + extra), 0)
    seq_block = me // groups
    wide_length = jnp.zeros((rows, cached_rows + extra), jnp.int32)
    for r in range(rows):
        wide_length = jnp.where(wide_row == r, length_ref[r], wide_length)
    own_cached = (
        (column < cached_rows)
        & ((column & (rows - 1)) == wide_row)
        & (seq_block * cached_rows + column < wide_length * rows)
    )
    fresh_column = column - cached_rows
    fresh_row = (fresh_column >= 0) & ((column & 15) == wide_row) & (seq_block == 0)

    for copy in small:
        copy.wait()
    for r in range(rows):
        adapter = adapter_ref[r]
        dq_s[pl.ds(r * rank, rank)] = qd_s[adapter]
        dv_s[pl.ds(r * rank, rank)] = vd_s[adapter]

    spread_column = lax.broadcasted_iota(jnp.int32, (rows, rows * rank), 1)
    spread_row = lax.broadcasted_iota(jnp.int32, (rows, rows * rank), 0)
    own_block = spread_column // rank == spread_row
    lane_block = lane // rank

    def contract(left, right):
        return lax.dot_general(
            left, right, (((1,), (1,)), ((), ())), preferred_element_type=f32
        )

    def fold(x):
        x = jnp.where(own_block, x, 0.0)
        parts = split_chunks(x)
        total = parts[0]
        for part in parts[1:]:
            total = total + part
        shift = hd // 2
        while shift >= rank:
            total = total + pltpu.roll(total, shift, 1)
            shift //= 2
        return total

    def send_shrink(t):
        scaled = (current * gains).astype(bf16)
        squares = jnp.sum(current * current, axis=1, keepdims=True)
        both = jnp.where(
            lane_block == 0,
            fold(contract(scaled, dq_s[...])),
            jnp.where(lane_block == 1, fold(contract(scaled, dv_s[...])), squares),
        )
        ssend[t] = both
        s_pair(t).start()

    send_shrink(0)

    for t in range(STEPS):
        if t == 0:
            for copies in weights:
                for copy in copies:
                    copy.wait()
        products = jnp.zeros((rows, q_cols + 2 * kv_cols), f32)

        def project(source):
            block = xg[t, source].astype(f32)
            parts = [block[c * rows : (c + 1) * rows] for c in range(chunks)]
            cols = pl.ds(pl.multiple_of(source * width, width), width)
            return contract(jnp.concatenate(parts, axis=1).astype(bf16), w_s[:, cols])

        for k in range(0, n, 2):
            source = flip(me, k)
            if k:
                x_copy(t, source, source).wait_recv()
                x_pass(t, source, sibling).start()
            products = products + project(source)
            if k == 2:
                s_pair(t).wait_recv()
                pair_sum = ssend[t] + sp[t]
                ssum[t] = pair_sum
                sg[t, me // 2] = pair_sum
                for other in range(2, n, 2):
                    s_copy(t, me, flip(me, other)).start()
        for k in range(1, n, 2):
            source = flip(me, k)
            x_copy(t, source, source).wait_recv()
            products = products + project(source)
        if t == 0:
            for copy in ups:
                copy.wait()
            for r in range(rows):
                adapter = adapter_ref[r]
                uq_s[pl.ds(r * rank, rank)] = qu_s[adapter]
                uv_s[pl.ds(r * rank, rank)] = vu_s[adapter]
        for k in range(2, n, 2):
            source = flip(me, k)
            s_copy(t, source, source).wait_recv()
        shrink = sg[t, 0]
        for d in range(1, n // 2):
            shrink = shrink + sg[t, d]
        squares = shrink[:, 2 * rank : 2 * rank + 1]
        inv_rms = lax.rsqrt(squares / MODEL_WIDTH + eps_norm)
        shrink = shrink * inv_rms

        def spread(kind):
            x = jnp.where(lane_block == kind, shrink, 0.0)
            shift = rank
            while shift < hd:
                x = x + pltpu.roll(x, shift, 1)
                shift *= 2
            x = jnp.concatenate([x] * (rows * rank // hd), axis=1)
            return jnp.where(own_block, x, 0.0).astype(bf16)

        q_low = spread(0)
        v_low = spread(1)
        products = products * inv_rms
        q_up = jnp.dot(q_low, uq_s[...], preferred_element_type=f32)
        v_up = jnp.dot(v_low, uv_s[...], preferred_element_type=f32)
        query = products[:, :q_cols] + adapter_scale * q_up
        fresh = products[:, q_cols:] + adapter_scale * jnp.concatenate(
            [jnp.zeros((rows, kv_cols), f32), v_up], axis=1
        )
        q_cos, q_sin, k_cos, k_sin = tables[t]
        parts = [rotate(part, q_cos, q_sin) for part in split_chunks(query)]
        parts.append(rotate(fresh, k_cos, k_sin))
        parts.append(jnp.zeros((rows, hd), f32))
        message = jnp.concatenate(parts, axis=0).astype(bf16)
        qsend[t] = message
        side = lax.rem(me, 2)
        for block in range(blocks):
            target = me // 2 + block * groups

            @pl.when(target == me)
            def _():
                qg[t, side] = message

            @pl.when(target != me)
            def _():
                q_copy(t, side, block, target).start()

        if t == 0:
            for copy in caches:
                copy.wait()
        for half in range(2):
            source = 2 * lax.rem(me, groups) + half

            @pl.when(source != me)
            def _():
                q_copy(t, half, 0, source).wait_recv()

        first = qg[t, 0].astype(f32)
        second = qg[t, 1].astype(f32)
        q_rows = heads_here * rows
        queries = jnp.concatenate([first[:q_rows], second[:q_rows]], axis=0).astype(bf16)
        first_kv = first[q_rows : q_rows + rows]
        second_kv = second[q_rows : q_rows + rows]
        key_new = jnp.where(is_key, first_kv, pltpu.roll(second_kv, kv_cols, 1))
        value_new = jnp.where(is_key, pltpu.roll(first_kv, kv_cols, 1), second_kv)
        blank = jnp.zeros((16 - rows, hd), f32)
        k_s[pl.ds(cached_rows + 16 * t, 16)] = jnp.concatenate([key_new, blank], 0).astype(bf16)
        v_s[pl.ds(cached_rows + 16 * t, 16)] = jnp.concatenate([value_new, blank], 0).astype(bf16)
        scores = contract(queries, k_s[...]) * (HEAD_DIMENSION ** (-0.5))
        scores = scores.reshape(per_group, rows, cached_rows + extra)
        live = (own_cached | (fresh_row & (fresh_column < 16 * (t + 1))))[None]
        scores = jnp.where(live, scores, big_negative)
        peak = jnp.max(scores, axis=2, keepdims=True)
        weight = jnp.where(live, jnp.exp(scores - peak), 0.0)
        mass = jnp.sum(weight, axis=2, keepdims=True)
        weight = weight.reshape(per_group * rows, cached_rows + extra).astype(bf16)
        summed = jnp.dot(weight, v_s[...], preferred_element_type=f32)
        summed = summed.reshape(per_group, rows, hd)
        some = mass > 0.0
        safe = jnp.where(some, mass, 1.0)
        partial = summed / safe
        level = jnp.where(some, peak + jnp.log(safe), big_negative)
        levels = jnp.zeros((rows, hd), f32)
        for h in range(per_group):
            levels = jnp.where(lane == h, level[h], levels)
        high = levels.astype(bf16).astype(f32)
        middle = (levels - high).astype(bf16).astype(f32)
        low = levels - high - middle
        packed = high + pltpu.roll(middle, per_group, 1) + pltpu.roll(low, 2 * per_group, 1)
        message = jnp.concatenate(
            [partial.reshape(per_group * rows, hd), packed, jnp.zeros((16 - rows, hd), f32)], axis=0
        ).astype(bf16)
        osend[t] = message
        og[t, me] = message
        for k in range(2, n, 2):
            o_copy(t, me, flip(me, k)).start()
        o_copy(t, me, sibling).start()
        if t == 0:
            for copy in out_weights:
                copy.wait()
        projected = jnp.zeros((rows, width), f32)
        own_group = lax.rem(me, groups)
        order = [k for k in range(groups) if k % 2 == 0] + [k for k in range(groups) if k % 2]
        for k in order:
            g = flip(own_group, k)
            found = []
            for b in range(blocks):
                source = b * groups + g
                if k % 2:
                    o_copy(t, source, source).wait_recv()
                elif k:
                    o_copy(t, source, source).wait_recv()
                    o_pass(t, source, sibling).start()
                else:

                    @pl.when(source != me)
                    def _():
                        o_copy(t, source, source).wait_recv()
                        o_pass(t, source, sibling).start()

            for b in range(blocks):
                entry = og[t, b * groups + g].astype(f32)
                packed = entry[per_group * rows : per_group * rows + rows]
                level = (
                    packed
                    + pltpu.roll(packed, hd - per_group, 1)
                    + pltpu.roll(packed, hd - 2 * per_group, 1)
                )
                found.append((level, entry))
            top = found[0][0]
            for level, _ in found[1:]:
                top = jnp.maximum(top, level)
            shares = [jnp.exp(level - top) for level, _ in found]
            whole = shares[0]
            for share in shares[1:]:
                whole = whole + share
            shares = [share / whole for share in shares]
            parts = []
            for h in range(per_group):
                value = jnp.zeros((rows, hd), f32)
                for share, (_, entry) in zip(shares, found):
                    value = value + share[:, h : h + 1] * entry[h * rows : (h + 1) * rows]
                parts.append(value)
            attention = jnp.concatenate(parts, axis=1).astype(bf16)
            wide = per_group * hd
            cols = pl.ds(pl.multiple_of(g * wide, wide), wide)
            projected = projected + contract(attention, wo_s[:, cols])
        rounded = (current + projected).astype(bf16)
        out_ref[t] = rounded
        current = rounded.astype(f32)
        if t + 1 < STEPS:
            send_state(t + 1)
            send_shrink(t + 1)

    for t in range(STEPS):
        x_copy(t, me, sibling).wait_send()
        s_pair(t).wait_send()
        for k in range(2, n, 2):
            other = flip(me, k)
            x_copy(t, me, other).wait_send()
            x_pass(t, other, sibling).wait_send()
            s_copy(t, me, other).wait_send()
            o_copy(t, me, other).wait_send()
            o_pass(t, other, sibling).wait_send()
        o_copy(t, me, sibling).wait_send()
        for block in range(blocks):
            target = me // 2 + block * groups

            @pl.when(target != me)
            def _():
                q_copy(t, 0, block, target).wait_send()


def fused(
    n,
    residual_input,
    attention_norm_gain,
    wq,
    wk,
    wv,
    wo,
    query_down_factor,
    query_up_factor,
    value_down_factor,
    value_up_factor,
    request_adapter,
    cached_lengths,
    rotated_key_cache,
    cached_value_rows,
):
    rows, width = residual_input.shape
    ctx_dev = rotated_key_cache.shape[0]
    q_cols, kv_cols = wq.shape[0], wk.shape[0]
    adapters, _, rank = query_down_factor.shape
    hd = HEAD_DIMENSION
    chunks = width // hd
    per_group = QUERY_HEADS // KEY_VALUE_HEADS
    blocks = n // KEY_VALUE_HEADS
    kv_rows = ctx_dev * rows + 128
    x_rows = chunks * rows
    q_rows = (q_cols // hd + 2) * rows
    o_rows = per_group * rows + 16
    bf16, f32 = jnp.bfloat16, jnp.float32
    dma = pltpu.SemaphoreType.DMA
    any_spec = pl.BlockSpec(memory_space=pl.ANY)
    vmem = pl.BlockSpec(memory_space=pltpu.VMEM)
    smem = pl.BlockSpec(memory_space=pltpu.SMEM)
    return pl.pallas_call(
        functools.partial(fused_kernel, n, ctx_dev),
        out_shape=jax.ShapeDtypeStruct((STEPS, rows, width), bf16),
        in_specs=[vmem, vmem, smem, smem] + [any_spec] * 10,
        out_specs=vmem,
        scratch_shapes=[
            pltpu.VMEM((q_cols + 2 * kv_cols, MODEL_WIDTH), bf16),
            pltpu.VMEM((width, MODEL_WIDTH), bf16),
            pltpu.VMEM((adapters, rank, width), bf16),
            pltpu.VMEM((adapters, rank, width), bf16),
            pltpu.VMEM((adapters, rank, q_cols), bf16),
            pltpu.VMEM((adapters, rank, kv_cols), bf16),
            pltpu.VMEM((kv_rows, hd), bf16),
            pltpu.VMEM((kv_rows, hd), bf16),
            pltpu.VMEM((rows * rank, width), bf16),
            pltpu.VMEM((rows * rank, width), bf16),
            pltpu.VMEM((rows * rank, q_cols), bf16),
            pltpu.VMEM((rows * rank, kv_cols), bf16),
            pltpu.VMEM((STEPS, n, x_rows, hd), bf16),
            pltpu.VMEM((STEPS, n // 2, rows, hd), f32),
            pltpu.VMEM((STEPS, rows, hd), f32),
            pltpu.VMEM((STEPS, 2, q_rows, hd), bf16),
            pltpu.VMEM((STEPS, n, o_rows, hd), bf16),
            pltpu.VMEM((STEPS, x_rows, hd), bf16),
            pltpu.VMEM((STEPS, rows, hd), f32),
            pltpu.VMEM((STEPS, rows, hd), f32),
            pltpu.VMEM((STEPS, q_rows, hd), bf16),
            pltpu.VMEM((STEPS, o_rows, hd), bf16),
            dma((24,)),
            dma((STEPS, n)),
            dma((STEPS, n)),
            dma((STEPS, n)),
            dma((STEPS, n // 2)),
            dma((STEPS, n // 2)),
            dma((STEPS, 2)),
            dma((STEPS, blocks)),
            dma((STEPS, 2)),
            dma((STEPS, n)),
            dma((STEPS, n)),
            dma((STEPS, n)),
        ],
        compiler_params=pltpu.CompilerParams(
            collective_id=0, has_side_effects=True, vmem_limit_bytes=56 * 1024 * 1024
        ),
    )(
        residual_input,
        attention_norm_gain,
        request_adapter,
        cached_lengths,
        wq,
        wk,
        wv,
        wo,
        jnp.swapaxes(query_down_factor, 1, 2),
        query_up_factor,
        jnp.swapaxes(value_down_factor, 1, 2),
        value_up_factor,
        rotated_key_cache.reshape(ctx_dev * rows, hd),
        cached_value_rows.reshape(ctx_dev * rows, hd),
    )


def solution(mesh):
    n = mesh.shape["tensor"]
    body = functools.partial(fused, n) if n == 2 * KEY_VALUE_HEADS else local
    in_specs = (
        P("parts", "tensor"),
        P("tensor"),
        P("tensor", None),
        P("tensor", None),
        P("tensor", None),
        P("tensor", None),
        P(None, "tensor", None),
        P(None, None, "tensor"),
        P(None, "tensor", None),
        P(None, None, "tensor"),
        P("parts"),
        P("parts"),
        P("tensor", "parts", None),
        P("tensor", "parts", None),
    )
    out_specs = P(None, "parts", "tensor")
    return jax.shard_map(body, mesh=mesh, in_specs=in_specs, out_specs=out_specs, check_vma=False)
```
